32 devices in a mesh: map: 4 (over z), gx: 4 (over x, core), gy: 2 (over y).
Axes of the slice: x: 2, y: 2, z: 4, core: 2. Of those that a mesh axis runs over, the one named last changes fastest.
Arguments:
- densities: float32 [4, 1536, 2048], P('map', 'gx', 'gy'), may hold values from 0.2 to 41, as said below
- scaling: float32 [4, 1536, 2048], P('map', 'gx', 'gy'), may hold values from 0.5 to 2
- weights: float32 [4], P('map'), as said below
Outputs:
- barycenter: float32 [1536, 2048], P('gx', 'gy')
- new_scaling: float32 [4, 1536, 2048], P('map', 'gx', 'gy')
The draws below stay inside these ranges and needn't reach their ends.
Inputs may be any that keep to these rules, and one draw needn't show every extreme that they name: `densities`: every cell's demand density is positive. The weights are positive and sum to one.
All inputs are finite; a program needn't handle non-finite values.
Results may differ from the reference program's by a relative error of at most 0.0001.
Values sent between devices are 32-bit elements; how exact they have to be, the bound alone decides.
No kernel may reach another device: no remote copies, remote signals or barrier semaphores. Data moves between devices by JAX's collectives and lax.ppermute only.
A program may use at most 64 MiB of HBM per device.

```python
import math
import jax
import jax.numpy as jnp
from jax import lax

HALF = 32
SIGMA = 16
NX = 1536
NY = 2048
MAPS = 4


def draw_densities(key, part):
    key_hour = jax.random.fold_in(key, 11)
    key_cell = jax.random.fold_in(key, 23)
    rows = jnp.arange(NX, dtype=jnp.float32) / jnp.float32(NX - 1)
    cols = jnp.arange(NY, dtype=jnp.float32) / jnp.float32(NY - 1)
    trend = (1.0 + 2.0 * rows)[:, None] * (1.0 + 2.0 * cols)[None, :]
    hour = jnp.exp(jax.random.uniform(key_hour, (MAPS, 1, 1), jnp.float32, -0.69, 0.69))
    rough = jnp.exp(jax.random.uniform(key_cell, (MAPS, NX, NY), jnp.float32, -0.8, 0.8))
    return (trend[None, :, :] * hour * rough).astype(jnp.float32)


def draw_weights(key, part):
    key_weight = jax.random.fold_in(key, 37)
    raw = jnp.exp(jax.random.uniform(key_weight, (MAPS,), jnp.float32, -0.69, 0.69))
    return (raw / jnp.sum(raw)).astype(jnp.float32)


def level_of(key, dims, shards, low, largest):
    level = 1.0
    for position, parts in shards:
        draws = jax.random.uniform(jax.random.fold_in(jax.random.fold_in(key, 6), position), (parts,), jnp.float32, low / len(shards), largest / len(shards))
        level = level * jnp.repeat(jnp.exp(draws), dims[position] // parts).reshape((-1,) + (1,) * (len(dims) - 1 - position))
    return level


def setup_inputs(seed: int = 0) -> dict:
    key_of = jax.random.split(jax.random.key(seed), 4)
    return {
        "densities": draw_densities(jax.random.fold_in(key_of[3], 71), 0),
        "scaling": jnp.clip(jnp.exp(math.log(2.0) - 1.3862944 * jax.random.uniform(key_of[1], (MAPS, NX, NY), jnp.float32) ** level_of(key_of[1], (MAPS, NX, NY), ((0, 4), (1, 4), (2, 2)), -0.2, 0.2)), 0.5, 2.0),
        "weights": draw_weights(jax.random.fold_in(key_of[3], 71), 0),
    }


def kernel_band(count):
    rows = jnp.arange(count, dtype=jnp.int32)[:, None]
    cols = jnp.arange(count + 2 * HALF, dtype=jnp.int32)[None, :]
    offset = (cols - rows - HALF).astype(jnp.float32)
    inside = jnp.abs(cols - rows - HALF) <= HALF
    taps = jnp.arange(2 * HALF + 1, dtype=jnp.float32) - HALF
    total = jnp.sum(jnp.exp(-taps * taps / (2.0 * SIGMA * SIGMA)))
    values = jnp.exp(-offset * offset / (2.0 * SIGMA * SIGMA)) / total
    return jnp.where(inside, values, jnp.float32(0.0))


def smooth_axis(padded, axis, length):
    block = min(128, length)
    nblocks = length // block
    pieces = -(-(block + 2 * HALF) // block)
    extra = (nblocks + pieces - 1) * block - (length + 2 * HALF)
    widths = [(0, 0)] * padded.ndim
    widths[axis] = (0, extra)
    padded = jnp.pad(padded, widths)
    band = kernel_band(block)
    band = jnp.pad(band, ((0, 0), (0, pieces * block - block - 2 * HALF)))
    result = None
    for index in range(pieces):
        piece = lax.slice_in_dim(padded, index * block, index * block + length, axis=axis)
        small = band[:, index * block:(index + 1) * block]
        if axis == 1:
            piece = piece.reshape(piece.shape[0], nblocks, block, piece.shape[2])
            term = jnp.einsum("ic,mbcj->mbij", small, piece, precision=lax.Precision.HIGHEST, preferred_element_type=jnp.float32)
        else:
            piece = piece.reshape(piece.shape[0], piece.shape[1], nblocks, block)
            term = jnp.einsum("mibc,kc->mibk", piece, small, precision=lax.Precision.HIGHEST, preferred_element_type=jnp.float32)
        result = term if result is None else result + term
    if axis == 1:
        return result.reshape(result.shape[0], length, result.shape[3])
    return result.reshape(result.shape[0], result.shape[1], length)


def convolve(field):
    stack = field[None, :, :]
    tall = jnp.pad(stack, ((0, 0), (HALF, HALF), (0, 0)))
    rows_done = smooth_axis(tall, 1, field.shape[0])
    broad = jnp.pad(rows_done, ((0, 0), (0, 0), (HALF, HALF)))
    return smooth_axis(broad, 2, field.shape[1])[0]


def reference(densities, scaling, weights):
    def per_map(items):
        density, scale, weight = items
        kv = convolve(scale)
        u_field = density / kv
        ku = convolve(u_field)
        return ku, weight * jnp.log(scale * ku)

    ku, terms = lax.map(per_map, (densities, scaling, weights))
    logsum = jnp.sum(terms, axis=0)
    raw = jnp.exp(logsum)
    mass = jnp.sum(raw)
    barycenter = jnp.float32(NX * NY) * raw / mass
    new_scaling = barycenter[None, :, :] / ku
    return barycenter, new_scaling
```

```python
import math

import jax
import jax.numpy as jnp
import numpy as np
from jax import lax
from jax.experimental import pallas as pl
from jax.experimental.pallas import tpu as pltpu
from jax.sharding import PartitionSpec as P

HALF = 32
SIGMA = 16
WIDE = 2 * HALF
LANES = 128
F32 = jnp.float32
BF16 = jnp.bfloat16


def gauss(offset):
    taps = np.arange(-HALF, HALF + 1, dtype=np.float64)
    total = np.exp(-taps * taps / (2.0 * SIGMA * SIGMA)).sum()
    values = np.exp(-offset * offset / (2.0 * SIGMA * SIGMA)) / total
    return np.where(np.abs(offset) <= HALF, values, 0.0)


def halves(values):
    high = values.astype(np.float32).astype(BF16)
    low = (values - high.astype(np.float64)).astype(np.float32).astype(BF16)
    return jnp.asarray(np.stack([high, low]))


def row_band(count):
    i = np.arange(count, dtype=np.float64)[:, None]
    c = np.arange(count + WIDE, dtype=np.float64)[None, :]
    return halves(gauss(c - HALF - i))


def col_band(rows, cols, shift):
    c = np.arange(rows, dtype=np.float64)[:, None]
    j = np.arange(cols, dtype=np.float64)[None, :]
    return halves(gauss(c - shift - j))


def split(x):
    high = x.astype(BF16)
    low = (x - high.astype(F32)).astype(BF16)
    return high, low


def mm(a, b):
    return jnp.dot(a, b, preferred_element_type=F32)


def rows_of(band, x):
    (bh, bl), (xh, xl) = band, split(x)
    return mm(bh, xh) + mm(bh, xl) + mm(bl, xh)


def times(parts, band):
    (xh, xl), (bh, bl) = parts, band
    return mm(xh, bh) + mm(xl, bh) + mm(xh, bl)


def cols_all(x, band):
    width = x.shape[1]
    xh, xl = split(x)
    out = []
    for start in range(0, width, 256):
        lo, hi = max(start - LANES, 0), min(start + 256 + LANES, width)
        top, bottom = lo - (start - LANES), hi - (start - LANES)
        out.append(times((xh[:, lo:hi], xl[:, lo:hi]), (band[0][top:bottom], band[1][top:bottom])))
    return jnp.concatenate(out, axis=1)


def cols_inner(x, band):
    width = x.shape[1]
    xh, xl = split(x)
    out = []
    for start in range(0, width - 2 * LANES, 256):
        stop = min(start + 512, width)
        n = stop - start - 2 * LANES
        out.append(times((xh[:, start:stop], xl[:, start:stop]), (band[0][: stop - start, :n], band[1][: stop - start, :n])))
    return jnp.concatenate(out, axis=1)


def quotient(dens, kv):
    return jnp.where(dens > 0.0, dens / kv, 0.0)


def strip(scal, dens, tband, cband):
    n = dens.shape[0]
    kv = cols_all(rows_of((tband[0][:n, : n + WIDE], tband[1][:n, : n + WIDE]), scal), cband)
    u = quotient(dens, kv)
    m = n - WIDE
    return cols_inner(rows_of((tband[0][:m, :n], tband[1][:m, :n]), u), cband)


def band_of(ref):
    return (ref[0], ref[1])


def log_term(weight, scal, ku):
    return weight * jnp.log(scal * ku)


def vmem():
    return pl.BlockSpec(memory_space=pltpu.VMEM)


def smem():
    return pl.BlockSpec(memory_space=pltpu.SMEM)


def rowblock(rows, cols, index):
    return pl.BlockSpec((1, rows, cols), lambda i: (0, index, 0))


def call(body, out, in_specs, flops, name):
    return pl.pallas_call(
        body,
        grid=(1,),
        out_shape=[jax.ShapeDtypeStruct(s, F32) for s in out],
        in_specs=in_specs,
        out_specs=[vmem()] * len(out),
        compiler_params=pltpu.CompilerParams(vmem_limit_bytes=48 * 1024 * 1024),
        cost_estimate=pl.CostEstimate(flops=flops, bytes_accessed=4 * 1024 * 1024, transcendentals=0),
        name=name,
    )


def inner_chunk(weights, scaling, densities, tband, cband, index, pieces, pack):
    rows, cols = scaling.shape[1:]

    def body(*refs):
        w, s0, s1, d0, d1, tb, cb = refs[:7]
        refs = refs[7:]
        scal = jnp.concatenate([s0[0], s1[0]], axis=0)
        dens = jnp.concatenate([d0[0], d1[0]], axis=0)
        if pack:
            sl, dl, up, down = refs[0], refs[1], refs[-2], refs[-1]
            refs = refs[2:-2]
            up[:WIDE] = s0[0, :WIDE]
            up[WIDE:] = d0[0, :HALF]
            down[:WIDE] = sl[0]
            down[WIDE:] = dl[0, HALF:]
        ku = strip(scal, dens[HALF:-HALF], band_of(tb), band_of(cb))
        term = log_term(w[0], scal[WIDE:-WIDE, LANES:-LANES], ku)
        size = LANES // pieces
        for k in range(pieces):
            refs[2 * k][...] = term[k * size : (k + 1) * size]
            refs[2 * k + 1][...] = ku[k * size : (k + 1) * size]

    inner = (LANES // pieces, cols - 2 * LANES)
    out = [inner] * (2 * pieces)
    specs = [smem()] + [rowblock(128, cols, index), rowblock(128, cols, index + 1)] * 2 + [vmem(), vmem()]
    args = [weights, scaling, scaling, densities, densities, tband, cband]
    if pack:
        out += [(WIDE + HALF, cols)] * 2
        last = rows // WIDE - 1
        specs += [rowblock(WIDE, cols, last)] * 2
        args += [scaling, densities]
    return call(body, out, specs, 4_000_000_000, "inner")(*args)


def edge_chunk(weights, scaling, densities, tband, cband, up, down):
    rows, cols = scaling.shape[1:]

    def body(w, s0, s1, d0, d1, tb, cb, hu, hd, term, ku):
        tb, cb = band_of(tb), band_of(cb)
        top = jnp.concatenate([hu[:WIDE], s0[0]], axis=0)
        dens = jnp.concatenate([hu[WIDE:], d0[0, : 128 - HALF]], axis=0)
        k = strip(top, dens, tb, cb)
        ku[:WIDE] = k
        term[:WIDE] = log_term(w[0], s0[0, :WIDE, LANES:-LANES], k)
        low = jnp.concatenate([s1[0], hd[:WIDE]], axis=0)
        dens = jnp.concatenate([d1[0, HALF:], hd[WIDE:]], axis=0)
        k = strip(low, dens, tb, cb)
        ku[WIDE:] = k
        term[WIDE:] = log_term(w[0], s1[0, WIDE:, LANES:-LANES], k)

    last = rows // 128 - 1
    specs = [smem()] + [rowblock(128, cols, 0), rowblock(128, cols, last)] * 2 + [vmem()] * 4
    out = [(2 * WIDE, cols - 2 * LANES)] * 2
    return call(body, out, specs, 4_000_000_000, "edge")(
        weights, scaling, scaling, densities, densities, tband, cband, up, down
    )


def colblock(rows, index):
    return pl.BlockSpec((1, rows, LANES), lambda i: (0, 0, index))


def colblock2(rows, index):
    return pl.BlockSpec((rows, LANES), lambda i: (0, index))


def side_pack(scaling, densities, up, down):
    rows, cols = scaling.shape[1:]
    tall = rows + 2 * WIDE
    last = cols // LANES - 1
    two = lax.axis_size("gy") == 2

    def body(sl, sr, dl, dr, ul, ur, ol, orr, *outs):
        lane = lax.broadcasted_iota(jnp.int32, (tall, LANES), 1)
        zero = jnp.zeros((HALF, LANES), F32)

        def tallest(s, d, u, o):
            scal = jnp.concatenate([u[:WIDE], s[0], o[:WIDE]], axis=0)
            dens = jnp.concatenate([zero, u[WIDE:], d[0], o[WIDE:], zero], axis=0)
            return scal, dens

        scal, dens = tallest(sl, dl, ul, ol)
        left = jnp.where(lane < WIDE, scal, pltpu.roll(dens, WIDE, 1))
        scal, dens = tallest(sr, dr, ur, orr)
        right = jnp.where(lane >= WIDE, scal, pltpu.roll(dens, HALF, 1))
        if two:
            outs[0][...] = jnp.where(lax.axis_index("gy") == 0, right, left)
        else:
            outs[0][...] = left
            outs[1][...] = right

    specs = [colblock(rows, 0), colblock(rows, last)] * 2 + [colblock2(WIDE + HALF, 0), colblock2(WIDE + HALF, last)] * 2
    out = [(tall, LANES)] * (1 if two else 2)
    return call(body, out, specs, 1_000_000, "side_pack")(scaling, scaling, densities, densities, up, up, down, down)


def side_chunk(weights, scaling, densities, tband, gband, up, down, from_left, from_right, pieces):
    rows, cols = scaling.shape[1:]
    tall = rows + 2 * WIDE
    blocks = cols // LANES
    two = lax.axis_size("gy") == 2

    def body(*refs):
        w, s, d, u, o = refs[0], refs[1:5], refs[5:9], refs[9:13], refs[13:17]
        tb, gb, hl, hr = refs[17:21]
        outs = refs[21:]
        lane = lax.broadcasted_iota(jnp.int32, (tall, LANES), 1)
        tb, gb = band_of(tb), band_of(gb)
        here = lax.axis_index("gy")
        left, right = hl[...], hr[...]
        if two:
            left = jnp.where(here == 0, 0.0, left)
            right = jnp.where(here == 0, right, 0.0)
        left_s = jnp.where(lane >= WIDE, left, 0.0)
        left_d = jnp.where(lane >= LANES - HALF, pltpu.roll(left, LANES - HALF, 1), 0.0)
        right_s = jnp.where(lane < WIDE, right, 0.0)
        right_d = jnp.where(lane < HALF, pltpu.roll(right, WIDE, 1), 0.0)

        def scal(k):
            return jnp.concatenate([u[k][:WIDE], s[k][0], o[k][:WIDE]], axis=0)

        def dens(k):
            return jnp.concatenate([u[k][WIDE:], d[k][0], o[k][WIDE:]], axis=0)

        def side(sx, dx):
            n = tall - WIDE
            kv = times(split(rows_of((tb[0][:n, :tall], tb[1][:n, :tall]), sx)), gb)
            ux = quotient(dx, kv)
            r = rows_of((tb[0][:rows, :n], tb[1][:rows, :n]), ux)
            return times(split(r), (gb[0][:, LANES : 2 * LANES], gb[1][:, LANES : 2 * LANES]))

        inner = slice(HALF, tall - HALF)
        k0 = side(
            jnp.concatenate([left_s, scal(0), scal(1)], axis=1),
            jnp.concatenate([left_d[inner], dens(0), dens(1)], axis=1),
        )
        k1 = side(
            jnp.concatenate([scal(2), scal(3), right_s], axis=1),
            jnp.concatenate([dens(2), dens(3), right_d[inner]], axis=1),
        )
        size = rows // pieces
        for p in range(pieces):
            part = slice(p * size, (p + 1) * size)
            outs[2 * p][:, :LANES] = log_term(w[0], s[0][0, part], k0[part])
            outs[2 * p][:, LANES:] = log_term(w[0], s[3][0, part], k1[part])
            outs[2 * p + 1][:, :LANES] = k0[part]
            outs[2 * p + 1][:, LANES:] = k1[part]

    which = [0, 1, blocks - 2, blocks - 1]
    specs = [smem()] + [colblock(rows, k) for k in which] * 2 + [colblock2(WIDE + HALF, k) for k in which] * 2
    specs += [vmem()] * 4
    args = [weights] + [scaling] * 4 + [densities] * 4 + [up] * 4 + [down] * 4 + [tband, gband, from_left, from_right]
    out = [(rows // pieces, 2 * LANES)] * (2 * pieces)
    return call(body, out, specs, 6_000_000_000, "sides")(*args)


def finish(held, landed, ku, mass):
    count = lax.axis_size("map")

    def body(*refs):
        held_ref, landed_ref, ku_ref = refs[:3]
        raw_ref, quot_ref, mass_ref = refs[-3:]
        z = lax.axis_index("map")
        middle = (z == count // 2 - 1) | (z == count // 2)
        raw = jnp.exp(jnp.where(middle, held_ref[...], landed_ref[...]))
        raw_ref[...] = raw
        quot_ref[...] = raw / ku_ref[...]
        rows, cols = raw.shape
        part = jnp.sum(raw.reshape(rows // 8, 8, cols), axis=0)
        total = part[:, :LANES]
        for k in range(1, cols // LANES):
            total = total + part[:, k * LANES : (k + 1) * LANES]
        if len(refs) == 7:
            total = total + refs[3][...]
        mass_ref[...] = total

    args = [held, landed, ku] + ([] if mass is None else [mass])
    return call(body, [held.shape, held.shape, (8, LANES)], [vmem()] * len(args), 4_000_000, "finish")(*args)


def sum_grid(mass):
    for axis in ("gx", "gy"):
        count = lax.axis_size(axis)
        if count & (count - 1):
            mass = lax.psum(mass, axis)
            continue
        step = 1
        while step < count:
            mass = mass + lax.ppermute(mass, axis, [(i, i ^ step) for i in range(count)])
            step *= 2
    return mass


def assemble(mass, places, raws, quots, rows, cols, cells):
    n = len(places)

    def body(*refs):
        mass_ref, raw, quot = refs[0], refs[1 : 1 + n], refs[1 + n : 1 + 2 * n]
        bary, new = refs[-2:]
        scale = cells / jnp.sum(mass_ref[...])
        for k, place in enumerate(places):
            for source, r0, c0, height, width, from_row, from_col in place:
                piece = (slice(from_row, from_row + height), slice(from_col, from_col + width))
                bary[r0 : r0 + height, c0 : c0 + width] = raw[k][piece] * scale
                new[0, r0 : r0 + height, c0 : c0 + width] = quot[k][piece] * scale

    return call(body, [(rows, cols), (1, rows, cols)], [vmem()] * (1 + 2 * n), 4_000_000, "assemble")(
        mass, *raws, *quots
    )


def after(value, *others):
    return lax.optimization_barrier((value,) + others)[0]


def local(densities, scaling, weights):
    rows, cols = scaling.shape[1:]
    tband = row_band(rows + WIDE)
    cband = col_band(512, 256, LANES)
    gband = col_band(3 * LANES, 3 * LANES, 0)
    count = lax.axis_size("map")
    half = count // 2
    cells = float(rows * cols * lax.axis_size("gx") * lax.axis_size("gy"))

    def inward(x):
        for hop in range(half - 1):
            x = x + lax.ppermute(x, "map", [(hop, hop + 1), (count - 1 - hop, count - 2 - hop)])
        return x

    def across(x):
        return x + lax.ppermute(x, "map", [(half - 1, half), (half, half - 1)])

    def outward(x):
        got = x
        z = lax.axis_index("map")
        for hop in range(half - 2, -1, -1):
            pairs = [(hop + 1, hop), (count - 2 - hop, count - 1 - hop)]
            new = lax.ppermute(x, "map", pairs)
            if hop:
                x = jnp.where((z == hop) | (z == count - 1 - hop), new, x)
                got = x
            else:
                got = jnp.where((z == 0) | (z == count - 1), new, got) if half > 2 else new
        return got

    gx = lax.axis_size("gx")
    forward = [(i, i + 1) for i in range(gx - 1)]
    backward = [(i + 1, i) for i in range(gx - 1)]

    chunks, places = [], []
    nblocks = rows // 128 - 1
    wide = cols - 2 * LANES
    first = inner_chunk(weights, scaling, densities, tband, cband, 0, 2, True)
    packed_up, packed_down = first[-2:]
    chunks += [first[0:2], first[2:4]]
    places += [[(0, WIDE, LANES, 64, wide, 0, 0)], [(0, WIDE + 64, LANES, 64, wide, 0, 0)]]
    down = lax.ppermute(packed_up, "gx", backward)
    up = lax.ppermute(packed_down, "gx", forward)
    for k in range(1, nblocks):
        chunks.append(inner_chunk(weights, scaling, densities, tband, cband, k, 1, False))
        places.append([(0, WIDE + 128 * k, LANES, 128, wide, 0, 0)])
    chunks.append(edge_chunk(weights, scaling, densities, tband, cband, up, down))
    places.append([(0, 0, LANES, WIDE, wide, 0, 0), (0, rows - WIDE, LANES, WIDE, wide, WIDE, 0)])
    packs = side_pack(scaling, densities, up, down)
    gy = lax.axis_size("gy")
    if gy == 2:
        from_left = from_right = lax.ppermute(packs[0], "gy", [(0, 1), (1, 0)])
    else:
        from_right = lax.ppermute(packs[0], "gy", [(i + 1, i) for i in range(gy - 1)])
        from_left = lax.ppermute(packs[1], "gy", [(i, i + 1) for i in range(gy - 1)])
    sides = side_chunk(weights, scaling, densities, tband, gband, up, down, from_left, from_right, 2)
    size = rows // 2
    for k in range(2):
        chunks.append(sides[2 * k : 2 * k + 2])
        places.append(
            [(0, k * size, 0, size, LANES, 0, 0), (0, k * size, cols - LANES, size, LANES, 0, LANES)]
        )

    mass = None
    raws, quots = [], []
    for term, ku in chunks:
        held = across(inward(term))
        landed = outward(held)
        raw, quot, mass = finish(held, landed, ku, mass)
        raws.append(raw)
        quots.append(quot)
    mass = sum_grid(mass)
    bary, new = assemble(mass, places, raws, quots, rows, cols, cells)
    return bary, new


def solution(mesh):
    placed = (P("map", "gx", "gy"), P("map", "gx", "gy"), P("map"))
    return jax.shard_map(
        local,
        mesh=mesh,
        in_specs=placed,
        out_specs=(P("gx", "gy"), P("map", "gx", "gy")),
        check_vma=False,
    )
```

```python
import jax
import jax.numpy as jnp
import numpy as np
from jax import lax
from jax.experimental import pallas as pl
from jax.experimental.pallas import tpu as pltpu
from jax.sharding import PartitionSpec as P

HALF = 32
SIGMA = 16
WIDE = 2 * HALF
LANES = 128
BLOCK = 192
LAG = 3
F32 = jnp.float32
BF16 = jnp.bfloat16


def inverse_total():
    taps = np.arange(-HALF, HALF + 1, dtype=np.float64)
    return float(1.0 / np.exp(-taps * taps / (2.0 * SIGMA * SIGMA)).sum())


def split(x):
    high = x.astype(BF16)
    low = (x - high.astype(F32)).astype(BF16)
    return high, low


def band(rows, cols, shift):
    r = lax.broadcasted_iota(jnp.int32, (rows, cols), 0)
    c = lax.broadcasted_iota(jnp.int32, (rows, cols), 1)
    off = (r - c - shift).astype(F32)
    values = jnp.exp(off * off * (-0.5 / (SIGMA * SIGMA))) * inverse_total()
    return split(jnp.where(jnp.abs(off) <= HALF, values, 0.0))


def mm(a, b):
    return jnp.dot(a, b, preferred_element_type=F32)


def times(left, right):
    (lh, ll), (rh, rl) = left, right
    return mm(lh, rh) + mm(ll, rh) + mm(lh, rl)


def part(pair, rows=slice(None), cols=slice(None)):
    return pair[0][rows, cols], pair[1][rows, cols]


def rows_of(tall, x):
    x = split(x)
    n = x[0].shape[0] - WIDE
    out = []
    for start in range(0, n, BLOCK):
        m = min(BLOCK, n - start)
        out.append(times(part(tall, slice(m), slice(m + WIDE)), part(x, slice(start, start + m + WIDE))))
    return out[0] if len(out) == 1 else jnp.concatenate(out, axis=0)


def cols_all(wide, x):
    width = x.shape[1]
    x = split(x)
    out = []
    for start in range(0, width, 256):
        lo, hi = max(start - LANES, 0), min(start + 256 + LANES, width)
        rows = slice(lo - (start - LANES), hi - (start - LANES))
        out.append(times(part(x, cols=slice(lo, hi)), part(wide, rows)))
    return jnp.concatenate(out, axis=1)


def cols_inner(wide, x):
    width = x.shape[1]
    x = split(x)
    out = []
    for start in range(0, width - 2 * LANES, 256):
        stop = min(start + 512, width)
        band_part = part(wide, slice(stop - start), slice(stop - start - 2 * LANES))
        out.append(times(part(x, cols=slice(start, stop)), band_part))
    return jnp.concatenate(out, axis=1)


def quotient(dens, kv):
    return jnp.where(dens > 0.0, dens / kv, 0.0)


def pair_of(ref):
    return ref[0], ref[1]


def log_term(weight, scal, ku):
    return weight * jnp.log(scal * ku)


def vmem():
    return pl.BlockSpec(memory_space=pltpu.VMEM)


def smem():
    return pl.BlockSpec(memory_space=pltpu.SMEM)


def hbm():
    return pl.BlockSpec(memory_space=pltpu.HBM)


def call(body, out, in_specs, name, deps=(), scratch=()):
    n = len(in_specs)

    def run(*refs):
        body(*refs[:n], *refs[n + len(deps) :])

    kernel = pl.pallas_call(
        run,
        out_shape=[jax.ShapeDtypeStruct(s, F32) if isinstance(s, tuple) else s for s in out],
        in_specs=list(in_specs) + [pl.BlockSpec(memory_space=pl.ANY)] * len(deps),
        out_specs=[vmem()] * len(out),
        scratch_shapes=list(scratch),
        compiler_params=pltpu.CompilerParams(vmem_limit_bytes=40 * 1024 * 1024),
        cost_estimate=pl.CostEstimate(flops=0, bytes_accessed=0, transcendentals=0),
        name=name,
    )
    return lambda *args: kernel(*args, *deps)


def first_chunk(weights, scaling, densities):
    rows, cols = scaling.shape[1:]
    tall_n, dens_n = 3 * WIDE, 2 * WIDE

    def body(w, s_hbm, d_hbm, term, ku, tall_ref, wide_ref, one, two, s, d, sems):
        odd = lax.rem(lax.axis_index("gx"), 2)
        ends = ((one, (1 - odd) * (rows - WIDE), (1 - odd) * (rows - HALF)), (two, odd * (rows - WIDE), odd * (rows - HALF)))
        copies = [
            pltpu.make_async_copy(s_hbm.at[0, pl.ds(0, tall_n)], s, sems.at[0]),
            pltpu.make_async_copy(d_hbm.at[0, pl.ds(HALF, dens_n)], d, sems.at[1]),
        ]
        for k, (ref, s_row, d_row) in enumerate(ends):
            s_row, d_row = pl.multiple_of(s_row, HALF), pl.multiple_of(d_row, HALF)
            copies.append(pltpu.make_async_copy(s_hbm.at[0, pl.ds(s_row, WIDE)], ref.at[pl.ds(0, WIDE)], sems.at[2 + 2 * k]))
            copies.append(pltpu.make_async_copy(d_hbm.at[0, pl.ds(d_row, HALF)], ref.at[pl.ds(WIDE, HALF)], sems.at[3 + 2 * k]))
        for copy in copies:
            copy.start()
        tall = band(BLOCK, BLOCK + WIDE, -HALF)
        wide = band(512, 256, LANES)
        tall_ref[0], tall_ref[1] = tall
        wide_ref[0], wide_ref[1] = wide
        copies[0].wait()
        kv = cols_all(wide, rows_of(tall, s[...]))
        copies[1].wait()
        u = quotient(d[...], kv)
        k = cols_inner(wide, rows_of(tall, u))
        ku[...] = k
        term[...] = log_term(w[0], s[WIDE : 2 * WIDE, LANES:-LANES], k)
        for copy in copies[2:]:
            copy.wait()

    inner = (WIDE, cols - 2 * LANES)
    pack = (WIDE + HALF, cols)
    bands = [jax.ShapeDtypeStruct((2, BLOCK, BLOCK + WIDE), BF16), jax.ShapeDtypeStruct((2, 512, 256), BF16)]
    scratch = [pltpu.VMEM((tall_n, cols), F32), pltpu.VMEM((dens_n, cols), F32), pltpu.SemaphoreType.DMA((6,))]
    return call(body, [inner, inner, *bands, pack, pack], [smem(), hbm(), hbm()], "first", (), scratch)(
        weights, scaling, densities
    )


def inner_chunks(weights, scaling, densities, tall, wide, deps):
    rows, cols = scaling.shape[1:]
    count = rows // WIDE - 3

    def body(w, s, d, tall_ref, wide_ref, *outs):
        tall, wide = pair_of(tall_ref), pair_of(wide_ref)
        kv = cols_all(wide, rows_of(tall, s[0, WIDE:]))
        u = quotient(d[0, WIDE + HALF : rows - HALF], kv)
        k = cols_inner(wide, rows_of(tall, u))
        term = log_term(w[0], s[0, 2 * WIDE : rows - WIDE, LANES:-LANES], k)
        for p in range(count):
            outs[2 * p][...] = term[p * WIDE : (p + 1) * WIDE]
            outs[2 * p + 1][...] = k[p * WIDE : (p + 1) * WIDE]

    out = [(WIDE, cols - 2 * LANES)] * (2 * count)
    return call(body, out, [smem()] + [vmem()] * 4, "inner", deps)(weights, scaling, densities, tall, wide)


def halo_rows(one, two, cols=slice(None)):
    here, count = lax.axis_index("gx"), lax.axis_size("gx")
    odd = lax.rem(here, 2) == 1
    near, far = one[:, cols], two[:, cols]
    far = jnp.where((here == 0) | (here == count - 1), 0.0, far)
    return jnp.where(odd, near, far), jnp.where(odd, far, near)


def edge_chunks(weights, scaling, densities, tall, wide, one, two, deps):
    rows, cols = scaling.shape[1:]

    def body(w, s, d, tall_ref, wide_ref, one_ref, two_ref, *outs):
        tall, wide = pair_of(tall_ref), pair_of(wide_ref)
        up, down = halo_rows(one_ref, two_ref)
        scal = (
            jnp.concatenate([up[:WIDE], s[0, : 2 * WIDE]], axis=0),
            jnp.concatenate([s[0, rows - 2 * WIDE :], down[:WIDE]], axis=0),
        )
        dens = jnp.concatenate([up[WIDE:], d[0, : 3 * HALF], d[0, rows - 3 * HALF :], down[WIDE:]], axis=0)
        kv = cols_all(wide, jnp.concatenate([rows_of(tall, x) for x in scal], axis=0))
        u = quotient(dens, kv)
        k = cols_inner(wide, jnp.concatenate([rows_of(tall, x) for x in (u[: 2 * WIDE], u[2 * WIDE :])], axis=0))
        for p, start in enumerate((0, rows - WIDE)):
            kp = k[p * WIDE : (p + 1) * WIDE]
            outs[2 * p][...] = log_term(w[0], s[0, start : start + WIDE, LANES:-LANES], kp)
            outs[2 * p + 1][...] = kp

    out = [(WIDE, cols - 2 * LANES)] * 4
    return call(body, out, [smem()] + [vmem()] * 6, "edges", deps)(
        weights, scaling, densities, tall, wide, one, two
    )


def side_pack(scaling, densities, one, two, deps):
    rows, cols = scaling.shape[1:]
    tall = rows + 2 * WIDE
    pair = lax.axis_size("gy") == 2

    def body(s, d, one_ref, two_ref, *outs):
        lane = lax.broadcasted_iota(jnp.int32, (tall, LANES), 1)
        zero = jnp.zeros((HALF, LANES), F32)

        def tallest(which):
            up, down = halo_rows(one_ref, two_ref, which)
            scal = jnp.concatenate([up[:WIDE], s[0, :, which], down[:WIDE]], axis=0)
            dens = jnp.concatenate([zero, up[WIDE:], d[0, :, which], down[WIDE:], zero], axis=0)
            return scal, dens

        scal, dens = tallest(slice(cols - LANES, cols))
        last = jnp.where(lane >= WIDE, scal, pltpu.roll(dens, HALF, 1))
        scal, dens = tallest(slice(0, LANES))
        first = jnp.where(lane < WIDE, scal, pltpu.roll(dens, WIDE, 1))
        if pair:
            outs[0][...] = jnp.where(lax.axis_index("gy") == 0, last, first)
        else:
            outs[0][...] = last
            outs[1][...] = first

    out = [(tall, LANES)] * (1 if pair else 2)
    return call(body, out, [vmem()] * 4, "side_pack", deps)(scaling, densities, one, two)


def side_chunks(weights, scaling, densities, tall, one, two, from_left, from_right, deps):
    rows, cols = scaling.shape[1:]
    long = rows + 2 * WIDE
    width = cols - 2 * LANES
    count = rows * 2 * LANES // (WIDE * width)
    blocks = width // (2 * LANES)
    pair = lax.axis_size("gy") == 2

    def body(w, s, d, tall_ref, one_ref, two_ref, left_ref, right_ref, *outs):
        tall = pair_of(tall_ref)
        short = band(BLOCK + WIDE, BLOCK, HALF)
        here, last = lax.axis_index("gy"), lax.axis_size("gy") - 1
        left = jnp.where(here == 0, 0.0, left_ref[...])
        right = jnp.where(here == last, 0.0, right_ref[...])
        lane = lax.broadcasted_iota(jnp.int32, (long, LANES), 1)
        inner = slice(HALF, long - HALF)

        def block(which):
            up, down = halo_rows(one_ref, two_ref, which)
            scal = jnp.concatenate([up[:WIDE], s[0, :, which], down[:WIDE]], axis=0)
            dens = jnp.concatenate([up[WIDE:], d[0, :, which], down[WIDE:]], axis=0)
            return pltpu.roll(scal, WIDE, 1), dens

        def side(scal, dens):
            kv = times(split(rows_of(tall, scal)), short)
            u = quotient(dens, kv)
            r = split(rows_of(tall, u))
            return times(r, part(short, slice(BLOCK), slice(LANES)))

        small = lane[inner]
        (s0, d0), (s1, d1) = block(slice(0, LANES)), block(slice(LANES, 2 * LANES))
        scal = jnp.concatenate([jnp.where(lane < WIDE, pltpu.roll(left, WIDE, 1), s0), jnp.where(lane < WIDE, s0, s1)], axis=1)
        d0, d1 = pltpu.roll(d0, HALF, 1), pltpu.roll(d1, HALF, 1)
        dens = jnp.concatenate(
            [jnp.where(small < HALF, left[inner], d0), jnp.where(small < HALF, d0, d1)[:, :WIDE]], axis=1
        )
        k0 = side(scal, dens)
        (s0, d0), (s1, d1) = block(slice(cols - 2 * LANES, cols - LANES)), block(slice(cols - LANES, cols))
        scal = jnp.concatenate([jnp.where(lane < WIDE, s0, s1), jnp.where(lane < WIDE, s1, pltpu.roll(right, WIDE, 1))], axis=1)
        d0, d1 = pltpu.roll(d0, HALF, 1), pltpu.roll(d1, HALF, 1)
        halo = pltpu.roll(right, LANES - HALF, 1)[inner]
        dens = jnp.concatenate(
            [jnp.where(small < HALF, d0, d1), jnp.where(small < HALF, d1, halo)[:, :WIDE]], axis=1
        )
        k1 = side(scal, dens)
        for p in range(count):
            for b in range(blocks):
                r = slice((p * blocks + b) * WIDE, (p * blocks + b + 1) * WIDE)
                c = 2 * LANES * b
                outs[2 * p][:, c : c + LANES] = log_term(w[0], s[0, r, :LANES], k0[r])
                outs[2 * p][:, c + LANES : c + 2 * LANES] = log_term(w[0], s[0, r, cols - LANES :], k1[r])
                outs[2 * p + 1][:, c : c + LANES] = k0[r]
                outs[2 * p + 1][:, c + LANES : c + 2 * LANES] = k1[r]

    out = [(WIDE, width)] * (2 * count)
    return call(body, out, [smem()] + [vmem()] * 7, "sides", deps)(
        weights, scaling, densities, tall, one, two, from_left, from_right
    )


def add(a, b, deps):
    def body(a_ref, b_ref, out_ref):
        out_ref[...] = a_ref[...] + b_ref[...]

    return call(body, [a.shape], [vmem()] * 2, "add", deps)(a, b)[0]


def in_middle():
    z = lax.axis_index("map")
    return (z == 1) | (z == 2)


def add_and_pass(a, b, term, deps):
    def body(a_ref, b_ref, term_ref, out_ref, send_ref):
        total = a_ref[...] + b_ref[...]
        out_ref[...] = total
        send_ref[...] = jnp.where(in_middle(), total, term_ref[...])

    return call(body, [a.shape, a.shape], [vmem()] * 3, "add_and_pass", deps)(a, b, term)


def finish(held, landed, ku, mass, deps):
    inputs = [held] + ([] if landed is None else [landed]) + [ku] + ([] if mass is None else [mass])
    n = len(inputs)

    def body(*refs):
        raw_ref, quot_ref, mass_ref = refs[n:]
        logs = refs[0][...]
        if landed is not None:
            logs = jnp.where(in_middle(), logs, refs[1][...])
        raw = jnp.exp(logs)
        raw_ref[...] = raw
        quot_ref[...] = raw / refs[1 if landed is None else 2][...]
        rows, cols = raw.shape
        total = jnp.sum(raw.reshape(rows // 8, 8, cols), axis=0)
        total = sum(total[:, k : k + LANES] for k in range(0, cols, LANES))
        mass_ref[...] = total if mass is None else total + refs[n - 1][...]

    return call(body, [held.shape, held.shape, (8, LANES)], [vmem()] * n, "finish", deps)(*inputs)


def sum_grid(mass):
    for axis in ("gx", "gy"):
        count = lax.axis_size(axis)
        if count & (count - 1):
            mass = lax.psum(mass, axis)
            continue
        step = 1
        while step < count:
            mass = mass + lax.ppermute(mass, axis, [(i, i ^ step) for i in range(count)])
            step *= 2
    return mass


def assemble(mass, places, raws, quots, rows, cols, cells):
    n = len(places)

    def body(*refs):
        mass_ref, raw, quot = refs[0], refs[1 : 1 + n], refs[1 + n : 1 + 2 * n]
        bary, new = refs[-2:]
        scale = cells / jnp.sum(mass_ref[...])
        for k, place in enumerate(places):
            for r0, c0, width, from_col in place:
                piece = (slice(None), slice(from_col, from_col + width))
                bary[r0 : r0 + WIDE, c0 : c0 + width] = raw[k][piece] * scale
                new[0, r0 : r0 + WIDE, c0 : c0 + width] = quot[k][piece] * scale

    return call(body, [(rows, cols), (1, rows, cols)], [vmem()] * (1 + 2 * n), "assemble")(mass, *raws, *quots)


def chunk_places(rows, cols):
    width = cols - 2 * LANES
    starts = list(range(WIDE, rows - WIDE, WIDE)) + [0, rows - WIDE]
    places = [[(r, LANES, width, 0)] for r in starts]
    blocks = width // (2 * LANES)
    for p in range(rows * 2 * LANES // (WIDE * width)):
        place = []
        for b in range(blocks):
            r = (p * blocks + b) * WIDE
            place += [(r, 0, LANES, 2 * LANES * b), (r, cols - LANES, LANES, 2 * LANES * b + LANES)]
        places.append(place)
    return places


def local(densities, scaling, weights):
    rows, cols = scaling.shape[1:]
    places = chunk_places(rows, cols)
    n = len(places)
    gx, gy = lax.axis_size("gx"), lax.axis_size("gy")
    cells = float(rows * cols * gx * gy)
    maps = lax.axis_size("map")
    chain = [()]

    def done(*values):
        chain[0] = (values[0],)
        return values

    near = [(i, i ^ 1) for i in range(gx)]
    far = []
    for i in range(gx):
        for j in range(gy):
            other = ((i + 1) // 2 * 2 - (1 if i % 2 == 0 else 0)) if 0 < i < gx - 1 else i
            far.append((i * gy + j, other * gy + (j if other != i else j ^ 1)))
    outer = [(0, 1), (1, 0), (2, 3), (3, 2)]
    middle = []
    for g in range(gx):
        middle += [(gx + g, 2 * gx + g), (2 * gx + g, gx + g), (g, g ^ 1), (3 * gx + g, 3 * gx + (g ^ 1))]

    term, ku, sent, crossed, held, got = [None] * n, [None] * n, [None] * n, [None] * n, [None] * n, [None] * (n + LAG)
    raws, quots, mass = [None] * n, [None] * n, [None]

    def outward(k, value):
        if maps == 4 and k < n + LAG:
            got[k] = lax.ppermute(value, "map", outer)

    def receive(k):
        if maps == 4:
            (sent[k],) = done(add(term[k], got[k], chain[0]))
            crossed[k] = lax.ppermute(sent[k], ("map", "gx"), middle)

    def total(k):
        if maps == 4:
            later = term[min(k + LAG, n - 1)]
            held[k], passed = done(*add_and_pass(sent[k], crossed[k], later, chain[0]))
            outward(k + LAG, passed)
        else:
            held[k] = lax.psum(term[k], "map")

    def close(k):
        raws[k], quots[k], mass[0] = finish(held[k], got[k + LAG], ku[k], mass[0], chain[0])
        done(mass[0])

    def take(first, values):
        for k in range(len(values) // 2):
            term[first + k], ku[first + k] = values[2 * k : 2 * k + 2]
        done(values[0])

    *values, tall, wide, one, two = first_chunk(weights, scaling, densities)
    take(0, values)
    outward(0, term[0])
    one = lax.ppermute(one, "gx", near)
    two = lax.ppermute(two, ("gx", "gy"), far)
    take(1, inner_chunks(weights, scaling, densities, tall, wide, chain[0]))
    for k in range(1, LAG):
        outward(k, term[k])
    receive(0)
    packs = done(*side_pack(scaling, densities, one, two, chain[0]))
    if gy == 2:
        from_left = from_right = lax.ppermute(packs[0], "gy", [(0, 1), (1, 0)])
    else:
        from_left = lax.ppermute(packs[0], "gy", [(i, i + 1) for i in range(gy - 1)])
        from_right = lax.ppermute(packs[1], "gy", [(i + 1, i) for i in range(gy - 1)])
    receive(1)
    inner_count = rows // WIDE - 2
    take(inner_count, edge_chunks(weights, scaling, densities, tall, wide, one, two, chain[0]))
    total(0)
    receive(2)
    total(1)
    take(
        inner_count + 2,
        side_chunks(weights, scaling, densities, tall, one, two, from_left, from_right, chain[0]),
    )
    for k in range(3, n):
        receive(k)
        if k >= LAG:
            close_k = k - LAG
        total(k - 1)
        close(close_k)
    total(n - 1)
    for k in range(n - LAG, n):
        close(k)
    bary, new = assemble(sum_grid(mass[0]), places, raws, quots, rows, cols, cells)
    return bary, new


def solution(mesh):
    placed = (P("map", "gx", "gy"), P("map", "gx", "gy"), P("map"))
    return jax.shard_map(
        local,
        mesh=mesh,
        in_specs=placed,
        out_specs=(P("gx", "gy"), P("map", "gx", "gy")),
        check_vma=False,
    )
```

```python
import jax
import jax.numpy as jnp
import numpy as np
from jax import lax
from jax.experimental import pallas as pl
from jax.experimental.pallas import tpu as pltpu
from jax.sharding import PartitionSpec as P

HALF = 32
SIGMA = 16
WIDE = 2 * HALF
LANES = 128
BLOCK = 192
LAG = 4
F32 = jnp.float32
BF16 = jnp.bfloat16


def inverse_total():
    taps = np.arange(-HALF, HALF + 1, dtype=np.float64)
    return float(1.0 / np.exp(-taps * taps / (2.0 * SIGMA * SIGMA)).sum())


def split(x):
    high = x.astype(BF16)
    low = (x - high.astype(F32)).astype(BF16)
    return high, low


def band(rows, cols, shift):
    r = lax.broadcasted_iota(jnp.int32, (rows, cols), 0)
    c = lax.broadcasted_iota(jnp.int32, (rows, cols), 1)
    off = (r - c - shift).astype(F32)
    values = jnp.exp(off * off * (-0.5 / (SIGMA * SIGMA))) * inverse_total()
    return split(jnp.where(jnp.abs(off) <= HALF, values, 0.0))


def mm(a, b):
    return jnp.dot(a, b, preferred_element_type=F32)


def times(left, right):
    (lh, ll), (rh, rl) = left, right
    return mm(jnp.concatenate([lh, lh, ll], axis=1), jnp.concatenate([rh, rl, rh], axis=0))


def part(pair, rows=slice(None), cols=slice(None)):
    return pair[0][rows, cols], pair[1][rows, cols]


def rows_of(tall, x):
    x = split(x)
    n = x[0].shape[0] - WIDE
    out = []
    for start in range(0, n, BLOCK):
        m = min(BLOCK, n - start)
        out.append(times(part(tall, slice(m), slice(m + WIDE)), part(x, slice(start, start + m + WIDE))))
    return out[0] if len(out) == 1 else jnp.concatenate(out, axis=0)


def cols_of(wide, x, padded):
    margin = 0 if padded else LANES
    width = x.shape[1]
    x = split(x)
    out = []
    for start in range(margin, width - margin, 256):
        lo, hi = max(start - LANES, 0), min(start + 256 + LANES, width)
        rows = slice(lo - (start - LANES), hi - (start - LANES))
        out.append(times(part(x, cols=slice(lo, hi)), part(wide, rows)))
    return jnp.concatenate(out, axis=1)


def quotient(dens, kv):
    return jnp.where(dens > 0.0, dens / kv, 0.0)


def pair_of(ref):
    return ref[0], ref[1]


def log_term(weight, scal, ku):
    return weight * jnp.log(scal * ku)


def vmem():
    return pl.BlockSpec(memory_space=pltpu.VMEM)


def smem():
    return pl.BlockSpec(memory_space=pltpu.SMEM)


def hbm():
    return pl.BlockSpec(memory_space=pltpu.HBM)


COST = {'finish_last': 2.0, 'add': 4.0, 'inner': 2.5, 'edges': 2.3, 'sides': 2.5}


def call(body, out, in_specs, name, deps=(), scratch=(), out_specs=None):
    n = len(in_specs)

    def run(*refs):
        body(*refs[:n], *refs[n + len(deps) :])

    kernel = pl.pallas_call(
        run,
        out_shape=[jax.ShapeDtypeStruct(s, F32) if isinstance(s, tuple) else s for s in out],
        in_specs=list(in_specs) + [pl.BlockSpec(memory_space=pl.ANY)] * len(deps),
        out_specs=out_specs or [vmem()] * len(out),
        scratch_shapes=list(scratch),
        compiler_params=pltpu.CompilerParams(vmem_limit_bytes=40 * 1024 * 1024),
        cost_estimate=pl.CostEstimate(flops=int(COST.get(name, 0) * 1e9), bytes_accessed=0, transcendentals=0),
        name=name,
    )
    return lambda *args: kernel(*args, *deps)


def fill_pack(s, d, pack, last):
    rows = s.shape[1]
    for start, x, n in ((0, s, WIDE), (WIDE, d, HALF)):
        pack[start : start + n] = jnp.where(last, x[0, rows - n :], x[0, :n])


def first_chunk(weights, scaling, densities):
    rows, cols = scaling.shape[1:]
    tall_n, dens_n = 3 * WIDE, 2 * WIDE

    def body(w, s_hbm, d_hbm, term, ku, tall_ref, wide_ref, s, d, near, sems):
        copies = []
        for start, stop in ((0, tall_n), (tall_n, rows)):
            for source, ref in ((s_hbm, s), (d_hbm, d)):
                piece = (0, pl.ds(start, stop - start))
                copies.append(pltpu.make_async_copy(source.at[piece], ref.at[piece], sems.at[len(copies)]))
        for copy in copies[:2]:
            copy.start()
        tall = band(BLOCK, BLOCK + WIDE, -HALF)
        wide = band(512, 256, LANES)
        tall_ref[0], tall_ref[1] = tall
        wide_ref[0], wide_ref[1] = wide
        copies[0].wait()
        for copy in copies[2:]:
            copy.start()
        kv = cols_of(wide, rows_of(tall, s[0, :tall_n]), True)
        copies[1].wait()
        u = quotient(d[0, HALF : HALF + dens_n], kv)
        k = cols_of(wide, rows_of(tall, u), False)
        ku[...] = k
        term[...] = log_term(w[0], s[0, WIDE : 2 * WIDE, LANES:-LANES], k)
        for copy in copies[2:]:
            copy.wait()
        fill_pack(s, d, near, lax.rem(lax.axis_index("gx"), 2) == 0)

    inner = (WIDE, cols - 2 * LANES)
    bands = [jax.ShapeDtypeStruct((2, BLOCK, BLOCK + WIDE), BF16), jax.ShapeDtypeStruct((2, 512, 256), BF16)]
    whole, pack = (1, rows, cols), (WIDE + HALF, cols)
    out = [inner, inner, *bands, whole, whole, pack]
    return call(body, out, [smem(), hbm(), hbm()], "first", (), [pltpu.SemaphoreType.DMA((4,))])(
        weights,
        pltpu.with_memory_space_constraint(scaling, pltpu.HBM),
        pltpu.with_memory_space_constraint(densities, pltpu.HBM),
    )


def inner_chunks(weights, scaling, densities, tall, wide, deps):
    rows, cols = scaling.shape[1:]
    count = rows // WIDE - 3

    def body(w, s, d, tall_ref, wide_ref, *outs):
        tall, wide = pair_of(tall_ref), pair_of(wide_ref)
        kv = cols_of(wide, rows_of(tall, s[0, WIDE:]), True)
        u = quotient(d[0, WIDE + HALF : rows - HALF], kv)
        k = cols_of(wide, rows_of(tall, u), False)
        term = log_term(w[0], s[0, 2 * WIDE : rows - WIDE, LANES:-LANES], k)
        for p in range(count):
            outs[2 * p][...] = term[p * WIDE : (p + 1) * WIDE]
            outs[2 * p + 1][...] = k[p * WIDE : (p + 1) * WIDE]
        fill_pack(s, d, outs[2 * count], lax.rem(lax.axis_index("gx"), 2) == 1)

    out = [(WIDE, cols - 2 * LANES)] * (2 * count) + [(WIDE + HALF, cols)]
    return call(body, out, [smem()] + [vmem()] * 4, "inner", deps)(weights, scaling, densities, tall, wide)


def halo_rows(one, two, cols=slice(None)):
    here, count = lax.axis_index("gx"), lax.axis_size("gx")
    odd = lax.rem(here, 2) == 1
    near, far = one[:, cols], two[:, cols]
    far = jnp.where((here == 0) | (here == count - 1), 0.0, far)
    return jnp.where(odd, near, far), jnp.where(odd, far, near)


def edge_chunks(weights, scaling, densities, tall, wide, one, two, deps):
    rows, cols = scaling.shape[1:]

    def body(w, s, d, tall_ref, wide_ref, one_ref, two_ref, *outs):
        tall, wide = pair_of(tall_ref), pair_of(wide_ref)
        up, down = halo_rows(one_ref, two_ref)
        scal = (
            jnp.concatenate([up[:WIDE], s[0, : 2 * WIDE]], axis=0),
            jnp.concatenate([s[0, rows - 2 * WIDE :], down[:WIDE]], axis=0),
        )
        dens = jnp.concatenate([up[WIDE:], d[0, : 3 * HALF], d[0, rows - 3 * HALF :], down[WIDE:]], axis=0)
        kv = cols_of(wide, jnp.concatenate([rows_of(tall, x) for x in scal], axis=0), True)
        u = quotient(dens, kv)
        k = cols_of(wide, jnp.concatenate([rows_of(tall, x) for x in (u[: 2 * WIDE], u[2 * WIDE :])], axis=0), False)
        for p, start in enumerate((0, rows - WIDE)):
            kp = k[p * WIDE : (p + 1) * WIDE]
            outs[2 * p][...] = log_term(w[0], s[0, start : start + WIDE, LANES:-LANES], kp)
            outs[2 * p + 1][...] = kp

    out = [(WIDE, cols - 2 * LANES)] * 4
    return call(body, out, [smem()] + [vmem()] * 6, "edges", deps)(
        weights, scaling, densities, tall, wide, one, two
    )


def side_pack(scaling, densities, one, two, deps):
    rows, cols = scaling.shape[1:]
    tall = rows + 2 * WIDE
    pair = lax.axis_size("gy") == 2

    def body(s, d, one_ref, two_ref, *outs):
        lane = lax.broadcasted_iota(jnp.int32, (tall, LANES), 1)
        zero = jnp.zeros((HALF, LANES), F32)

        def tallest(which):
            up, down = halo_rows(one_ref, two_ref, which)
            scal = jnp.concatenate([up[:WIDE], s[0, :, which], down[:WIDE]], axis=0)
            dens = jnp.concatenate([zero, up[WIDE:], d[0, :, which], down[WIDE:], zero], axis=0)
            return scal, dens

        scal, dens = tallest(slice(cols - LANES, cols))
        last = jnp.where(lane >= WIDE, scal, pltpu.roll(dens, HALF, 1))
        scal, dens = tallest(slice(0, LANES))
        first = jnp.where(lane < WIDE, scal, pltpu.roll(dens, WIDE, 1))
        if pair:
            outs[0][...] = jnp.where(lax.axis_index("gy") == 0, last, first)
        else:
            outs[0][...] = last
            outs[1][...] = first

    out = [(tall, LANES)] * (1 if pair else 2)
    return call(body, out, [vmem()] * 4, "side_pack", deps)(scaling, densities, one, two)


def side_chunks(weights, scaling, densities, tall, one, two, from_left, from_right, deps):
    rows, cols = scaling.shape[1:]
    long = rows + 2 * WIDE
    width = cols - 2 * LANES
    count = rows * 2 * LANES // (WIDE * width)
    blocks = width // (2 * LANES)
    pair = lax.axis_size("gy") == 2

    def body(w, s, d, tall_ref, one_ref, two_ref, left_ref, right_ref, *outs):
        tall = pair_of(tall_ref)
        short = band(BLOCK + WIDE, BLOCK, HALF)
        here, last = lax.axis_index("gy"), lax.axis_size("gy") - 1
        left = jnp.where(here == 0, 0.0, left_ref[...])
        right = jnp.where(here == last, 0.0, right_ref[...])
        lane = lax.broadcasted_iota(jnp.int32, (long, LANES), 1)
        inner = slice(HALF, long - HALF)

        def block(which):
            up, down = halo_rows(one_ref, two_ref, which)
            scal = jnp.concatenate([up[:WIDE], s[0, :, which], down[:WIDE]], axis=0)
            dens = jnp.concatenate([up[WIDE:], d[0, :, which], down[WIDE:]], axis=0)
            return pltpu.roll(scal, WIDE, 1), dens

        def cols_of_both(sides, band):
            y = times(split(jnp.concatenate(sides, axis=0)), band)
            n = sides[0].shape[0]
            return y[:n], y[n:]

        small = lane[inner]
        (s0, d0), (s1, d1) = block(slice(0, LANES)), block(slice(LANES, 2 * LANES))
        scal = jnp.concatenate([jnp.where(lane < WIDE, pltpu.roll(left, WIDE, 1), s0), jnp.where(lane < WIDE, s0, s1)], axis=1)
        d0, d1 = pltpu.roll(d0, HALF, 1), pltpu.roll(d1, HALF, 1)
        dens = jnp.concatenate(
            [jnp.where(small < HALF, left[inner], d0), jnp.where(small < HALF, d0, d1)[:, :WIDE]], axis=1
        )
        first = scal, dens
        (s0, d0), (s1, d1) = block(slice(cols - 2 * LANES, cols - LANES)), block(slice(cols - LANES, cols))
        scal = jnp.concatenate([jnp.where(lane < WIDE, s0, s1), jnp.where(lane < WIDE, s1, pltpu.roll(right, WIDE, 1))], axis=1)
        d0, d1 = pltpu.roll(d0, HALF, 1), pltpu.roll(d1, HALF, 1)
        halo = pltpu.roll(right, LANES - HALF, 1)[inner]
        dens = jnp.concatenate(
            [jnp.where(small < HALF, d0, d1), jnp.where(small < HALF, d1, halo)[:, :WIDE]], axis=1
        )
        both = first, (scal, dens)
        kv = cols_of_both([rows_of(tall, scal) for scal, _ in both], short)
        u = [quotient(dens, x) for (_, dens), x in zip(both, kv)]
        k0, k1 = cols_of_both([rows_of(tall, x) for x in u], part(short, slice(BLOCK), slice(LANES)))
        for p in range(count):
            for b in range(blocks):
                r = slice((p * blocks + b) * WIDE, (p * blocks + b + 1) * WIDE)
                c = 2 * LANES * b
                outs[2 * p][:, c : c + LANES] = log_term(w[0], s[0, r, :LANES], k0[r])
                outs[2 * p][:, c + LANES : c + 2 * LANES] = log_term(w[0], s[0, r, cols - LANES :], k1[r])
                outs[2 * p + 1][:, c : c + LANES] = k0[r]
                outs[2 * p + 1][:, c + LANES : c + 2 * LANES] = k1[r]

    out = [(WIDE, width)] * (2 * count)
    return call(body, out, [smem()] + [vmem()] * 7, "sides", deps)(
        weights, scaling, densities, tall, one, two, from_left, from_right
    )


def add(a, b, deps, name="add"):
    def body(a_ref, b_ref, out_ref):
        out_ref[...] = a_ref[...] + b_ref[...]

    return call(body, [a.shape], [vmem()] * 2, name, deps)(a, b)[0]


def in_middle():
    z = lax.axis_index("map")
    return (z == 1) | (z == 2)


def mass_of(raw, mass_ref):
    rows, cols = raw.shape
    total = jnp.sum(raw.reshape(rows // 8, 8, cols), axis=0)
    total = sum(total[:, k : k + LANES] for k in range(0, cols, LANES))
    return total if mass_ref is None else total + mass_ref[...]


def add_and_pass(a, b, term, mass, deps):
    inputs = [a, b, term] + ([] if mass is None else [mass])
    n = len(inputs)

    def body(*refs):
        out_ref, send_ref, mass_ref = refs[n:]
        total = refs[0][...] + refs[1][...]
        out_ref[...] = total
        send_ref[...] = jnp.where(in_middle(), total, refs[2][...])
        mass_ref[...] = mass_of(jnp.exp(total), None if mass is None else refs[3])

    return call(body, [a.shape, a.shape, (8, LANES)], [vmem()] * n, "add_and_pass", deps)(*inputs)


def weigh(logs, mass, deps):
    inputs = [logs] + ([] if mass is None else [mass])
    n = len(inputs)

    def body(*refs):
        refs[n][...] = mass_of(jnp.exp(refs[0][...]), None if mass is None else refs[1])

    return call(body, [(8, LANES)], [vmem()] * n, "weigh", deps)(*inputs)


def finish(held, landed, ku, deps, name="finish"):
    inputs = [held] + ([] if landed is None else [landed]) + [ku]
    n = len(inputs)

    def body(*refs):
        raw_ref, quot_ref = refs[n:]
        logs = refs[0][...]
        if landed is not None:
            logs = jnp.where(in_middle(), logs, refs[1][...])
        raw = jnp.exp(logs)
        raw_ref[...] = raw
        quot_ref[...] = raw / refs[n - 1][...]

    return call(body, [held.shape, held.shape], [vmem()] * n, name, deps)(*inputs)


def sum_grid(mass, axes):
    for axis in axes:
        count = lax.axis_size(axis)
        if count & (count - 1):
            mass = lax.psum(mass, axis)
            continue
        step = 1
        while step < count:
            mass = mass + lax.ppermute(mass, axis, [(i, i ^ step) for i in range(count)])
            step *= 2
    return mass


def assemble(masses, places, raws, quots, rows, cols, cells):
    n, m = len(places), len(masses)

    def body(*refs):
        mass, raw, quot = refs[:m], refs[m : m + n], refs[m + n : m + 2 * n]
        bary_hbm, new_hbm, bary, new, sems = refs[m + 2 * n :]
        total = mass[0][...]
        if m > 1:
            total = jnp.where(in_middle(), total + mass[1][...], mass[2][...] + mass[3][...])
        scale = cells / jnp.sum(total)
        copies = []
        for row in range(0, rows, WIDE):
            band_rows = pl.ds(row, WIDE)
            for k, place in enumerate(places):
                for r0, c0, width, from_col in place:
                    if r0 == row:
                        piece = (slice(None), slice(from_col, from_col + width))
                        bary[row : row + WIDE, c0 : c0 + width] = raw[k][piece] * scale
                        new[row : row + WIDE, c0 : c0 + width] = quot[k][piece] * scale
            for source, target in ((bary, bary_hbm.at[band_rows]), (new, new_hbm.at[0, band_rows])):
                copies.append(pltpu.make_async_copy(source.at[band_rows], target, sems.at[len(copies)]))
                copies[-1].start()
        for copy in copies:
            copy.wait()

    tile = pltpu.VMEM((rows, cols), F32)
    return call(
        body,
        [(rows, cols), (1, rows, cols)],
        [vmem()] * (m + 2 * n),
        "assemble",
        scratch=[tile, tile, pltpu.SemaphoreType.DMA((2 * rows // WIDE,))],
        out_specs=[pl.BlockSpec(memory_space=pl.ANY)] * 2,
    )(*masses, *raws, *quots)


def chunk_places(rows, cols):
    width = cols - 2 * LANES
    starts = list(range(WIDE, rows - WIDE, WIDE)) + [0, rows - WIDE]
    places = [[(r, LANES, width, 0)] for r in starts]
    blocks = width // (2 * LANES)
    for p in range(rows * 2 * LANES // (WIDE * width)):
        place = []
        for b in range(blocks):
            r = (p * blocks + b) * WIDE
            place += [(r, 0, LANES, 2 * LANES * b), (r, cols - LANES, LANES, 2 * LANES * b + LANES)]
        places.append(place)
    return places


def local(densities, scaling, weights):
    rows, cols = scaling.shape[1:]
    places = chunk_places(rows, cols)
    n = len(places)
    gx, gy = lax.axis_size("gx"), lax.axis_size("gy")
    cells = float(rows * cols * gx * gy)
    maps = lax.axis_size("map")
    chain = [()]

    def done(*values):
        chain[0] = (values[0],)
        return values

    near = [(i, i ^ 1) for i in range(gx)]
    far = []
    for i in range(gx):
        for j in range(gy):
            other = ((i + 1) // 2 * 2 - (1 if i % 2 == 0 else 0)) if 0 < i < gx - 1 else i
            far.append((i * gy + j, other * gy + (j if other != i else j ^ 1)))
    outer = [(0, 1), (1, 0), (2, 3), (3, 2)]
    middle = []
    for g in range(gx):
        middle += [(gx + g, 2 * gx + g), (2 * gx + g, gx + g), (g, g ^ 1), (3 * gx + g, 3 * gx + (g ^ 1))]

    term, ku, sent, crossed, held, got = [None] * n, [None] * n, [None] * n, [None] * n, [None] * n, [None] * (n + LAG)
    raws, quots, mass = [None] * n, [None] * n, [None]

    def outward(k, value):
        if maps == 4 and k < n + LAG:
            got[k] = lax.ppermute(value, "map", outer)

    def receive(k):
        if maps == 4:
            (sent[k],) = done(add(term[k], got[k], chain[0]))
            crossed[k] = lax.ppermute(sent[k], ("map", "gx"), middle)

    def total(k):
        if maps == 4:
            later = term[min(k + LAG, n - 1)]
            held[k], passed, mass[0] = done(*add_and_pass(sent[k], crossed[k], later, mass[0], chain[0]))
            outward(k + LAG, passed)
        else:
            held[k] = lax.psum(term[k], "map")
            (mass[0],) = done(*weigh(held[k], mass[0], chain[0]))

    def close(k, name="finish"):
        raws[k], quots[k] = done(*finish(held[k], got[k + LAG], ku[k], chain[0], name))

    def take(first, values):
        for k in range(len(values) // 2):
            term[first + k], ku[first + k] = values[2 * k : 2 * k + 2]
        done(values[0])

    *values, tall, wide, scaling, densities, one = first_chunk(weights, scaling, densities)
    take(0, values)
    outward(0, term[0])
    one = lax.ppermute(one, "gx", near)
    *values, two = inner_chunks(weights, scaling, densities, tall, wide, (one,))
    take(1, values)
    for k in range(1, LAG):
        outward(k, term[k])
    two = lax.ppermute(two, ("gx", "gy"), far)
    receive(0)
    packs = done(*side_pack(scaling, densities, one, two, chain[0]))
    if gy == 2:
        from_left = from_right = lax.ppermute(packs[0], "gy", [(0, 1), (1, 0)])
    else:
        from_left = lax.ppermute(packs[0], "gy", [(i, i + 1) for i in range(gy - 1)])
        from_right = lax.ppermute(packs[1], "gy", [(i + 1, i) for i in range(gy - 1)])
    receive(1)
    inner_count = rows // WIDE - 2
    take(inner_count, edge_chunks(weights, scaling, densities, tall, wide, one, two, chain[0]))
    total(0)
    receive(2)
    total(1)
    receive(3)
    take(
        inner_count + 2,
        side_chunks(weights, scaling, densities, tall, one, two, from_left, from_right, chain[0]),
    )
    total(2)
    for k in range(4, n):
        receive(k)
        total(k - 1)
        close(k - LAG)
    close(n - LAG)
    total(n - 1)
    if maps == 4 and gx == 4 and gy == 2:
        own = sum_grid(mass[0], ("gx",))
        swap = [(i * gy + j, (i ^ 1) * gy + 1 - j) for i in range(4) for j in range(gy)]
        masses = [
            own,
            lax.ppermute(own, "gy", [(0, 1), (1, 0)]),
            lax.ppermute(own, "map", outer),
            lax.ppermute(own, ("map", "gy"), swap),
        ]
        for k in range(n - 3, n):
            close(k, "finish_last")
    else:
        masses = [sum_grid(mass[0], ("gx", "gy"))]
        if maps == 4:
            masses = [jnp.where(in_middle(), masses[0], lax.ppermute(masses[0], "map", outer))]
        for k in range(n - 3, n):
            close(k)
    bary, new = assemble(masses, places, raws, quots, rows, cols, cells)
    return bary, new


def solution(mesh):
    placed = (P("map", "gx", "gy"), P("map", "gx", "gy"), P("map"))
    return jax.shard_map(
        local,
        mesh=mesh,
        in_specs=placed,
        out_specs=(P("gx", "gy"), P("map", "gx", "gy")),
        check_vma=False,
    )
```

```python
import jax
import jax.numpy as jnp
import numpy as np
from jax import lax
from jax.experimental import pallas as pl
from jax.experimental.pallas import tpu as pltpu
from jax.sharding import PartitionSpec as P

HALF = 32
SIGMA = 16
WIDE = 2 * HALF
LANES = 128
BLOCK = 192
LAG = 4
F32 = jnp.float32
BF16 = jnp.bfloat16


def inverse_total():
    taps = np.arange(-HALF, HALF + 1, dtype=np.float64)
    return float(1.0 / np.exp(-taps * taps / (2.0 * SIGMA * SIGMA)).sum())


def split(x):
    high = x.astype(BF16)
    low = (x - high.astype(F32)).astype(BF16)
    return high, low


def band(rows, cols, shift):
    r = lax.broadcasted_iota(jnp.int32, (rows, cols), 0)
    c = lax.broadcasted_iota(jnp.int32, (rows, cols), 1)
    off = (r - c - shift).astype(F32)
    values = jnp.exp(off * off * (-0.5 / (SIGMA * SIGMA))) * inverse_total()
    return split(jnp.where(jnp.abs(off) <= HALF, values, 0.0))


def mm(a, b):
    return jnp.dot(a, b, preferred_element_type=F32)


def times(left, right):
    (lh, ll), (rh, rl) = left, right
    return mm(jnp.concatenate([lh, lh, ll], axis=1), jnp.concatenate([rh, rl, rh], axis=0))


def part(pair, rows=slice(None), cols=slice(None)):
    return pair[0][rows, cols], pair[1][rows, cols]


def rows_of(tall, x):
    x = split(x)
    n = x[0].shape[0] - WIDE
    out = []
    for start in range(0, n, BLOCK):
        m = min(BLOCK, n - start)
        out.append(times(part(tall, slice(m), slice(m + WIDE)), part(x, slice(start, start + m + WIDE))))
    return out[0] if len(out) == 1 else jnp.concatenate(out, axis=0)


def cols_of(wide, x, padded):
    margin = 0 if padded else LANES
    width = x.shape[1]
    x = split(x)
    out = []
    for start in range(margin, width - margin, 256):
        lo, hi = max(start - LANES, 0), min(start + 256 + LANES, width)
        rows = slice(lo - (start - LANES), hi - (start - LANES))
        out.append(times(part(x, cols=slice(lo, hi)), part(wide, rows)))
    return jnp.concatenate(out, axis=1)


def quotient(dens, kv):
    return jnp.where(dens > 0.0, dens / kv, 0.0)


def pair_of(ref):
    return ref[0], ref[1]


def log_term(weight, scal, ku):
    return weight * jnp.log(scal * ku)


def vmem():
    return pl.BlockSpec(memory_space=pltpu.VMEM)


def smem():
    return pl.BlockSpec(memory_space=pltpu.SMEM)


def hbm():
    return pl.BlockSpec(memory_space=pltpu.HBM)


COST = {'finish_last': 2.0, 'add': 4.0, 'inner': 2.5, 'edges': 2.3, 'sides': 2.5}


def call(body, out, in_specs, name, deps=(), scratch=(), out_specs=None):
    n = len(in_specs)

    def run(*refs):
        body(*refs[:n], *refs[n + len(deps) :])

    kernel = pl.pallas_call(
        run,
        out_shape=[jax.ShapeDtypeStruct(s, F32) if isinstance(s, tuple) else s for s in out],
        in_specs=list(in_specs) + [pl.BlockSpec(memory_space=pl.ANY)] * len(deps),
        out_specs=out_specs or [vmem()] * len(out),
        scratch_shapes=list(scratch),
        compiler_params=pltpu.CompilerParams(vmem_limit_bytes=40 * 1024 * 1024),
        cost_estimate=pl.CostEstimate(flops=int(COST.get(name, 0) * 1e9), bytes_accessed=0, transcendentals=0),
        name=name,
    )
    return lambda *args: kernel(*args, *deps)


def fill_pack(s, d, pack, last):
    rows = s.shape[1]
    for start, x, n in ((0, s, WIDE), (WIDE, d, HALF)):
        pack[start : start + n] = jnp.where(last, x[0, rows - n :], x[0, :n])


def first_chunk(weights, scaling, densities):
    rows, cols = scaling.shape[1:]
    tall_n, dens_n = 3 * WIDE, 2 * WIDE

    def body(w, s_hbm, d_hbm, term, ku, tall_ref, wide_ref, s, d, near, sems):
        copies = []
        for start, stop in ((0, tall_n), (tall_n, rows)):
            for source, ref in ((s_hbm, s), (d_hbm, d)):
                piece = (0, pl.ds(start, stop - start))
                copies.append(pltpu.make_async_copy(source.at[piece], ref.at[piece], sems.at[len(copies)]))
        for copy in copies[:2]:
            copy.start()
        tall = band(BLOCK, BLOCK + WIDE, -HALF)
        wide = band(512, 256, LANES)
        tall_ref[0], tall_ref[1] = tall
        wide_ref[0], wide_ref[1] = wide
        copies[0].wait()
        for copy in copies[2:]:
            copy.start()
        kv = cols_of(wide, rows_of(tall, s[0, :tall_n]), True)
        copies[1].wait()
        u = quotient(d[0, HALF : HALF + dens_n], kv)
        k = cols_of(wide, rows_of(tall, u), False)
        ku[...] = k
        term[...] = log_term(w[0], s[0, WIDE : 2 * WIDE, LANES:-LANES], k)
        for copy in copies[2:]:
            copy.wait()
        fill_pack(s, d, near, lax.rem(lax.axis_index("gx"), 2) == 0)

    inner = (WIDE, cols - 2 * LANES)
    bands = [jax.ShapeDtypeStruct((2, BLOCK, BLOCK + WIDE), BF16), jax.ShapeDtypeStruct((2, 512, 256), BF16)]
    whole, pack = (1, rows, cols), (WIDE + HALF, cols)
    out = [inner, inner, *bands, whole, whole, pack]
    return call(body, out, [smem(), hbm(), hbm()], "first", (), [pltpu.SemaphoreType.DMA((4,))])(
        weights,
        pltpu.with_memory_space_constraint(scaling, pltpu.HBM),
        pltpu.with_memory_space_constraint(densities, pltpu.HBM),
    )


def inner_chunks(weights, scaling, densities, tall, wide, deps):
    rows, cols = scaling.shape[1:]
    count = rows // WIDE - 3

    def body(w, s, d, tall_ref, wide_ref, *outs):
        tall, wide = pair_of(tall_ref), pair_of(wide_ref)
        kv = cols_of(wide, rows_of(tall, s[0, WIDE:]), True)
        u = quotient(d[0, WIDE + HALF : rows - HALF], kv)
        k = cols_of(wide, rows_of(tall, u), False)
        term = log_term(w[0], s[0, 2 * WIDE : rows - WIDE, LANES:-LANES], k)
        for p in range(count):
            outs[2 * p][...] = term[p * WIDE : (p + 1) * WIDE]
            outs[2 * p + 1][...] = k[p * WIDE : (p + 1) * WIDE]
        fill_pack(s, d, outs[2 * count], lax.rem(lax.axis_index("gx"), 2) == 1)

    out = [(WIDE, cols - 2 * LANES)] * (2 * count) + [(WIDE + HALF, cols)]
    return call(body, out, [smem()] + [vmem()] * 4, "inner", deps)(weights, scaling, densities, tall, wide)


def halo_rows(one, two, cols=slice(None)):
    here, count = lax.axis_index("gx"), lax.axis_size("gx")
    odd = lax.rem(here, 2) == 1
    near, far = one[:, cols], two[:, cols]
    far = jnp.where((here == 0) | (here == count - 1), 0.0, far)
    return jnp.where(odd, near, far), jnp.where(odd, far, near)


def edge_chunks(weights, scaling, densities, tall, wide, one, two, deps):
    rows, cols = scaling.shape[1:]

    def body(w, s, d, tall_ref, wide_ref, one_ref, two_ref, *outs):
        tall, wide = pair_of(tall_ref), pair_of(wide_ref)
        up, down = halo_rows(one_ref, two_ref)
        scal = (
            jnp.concatenate([up[:WIDE], s[0, : 2 * WIDE]], axis=0),
            jnp.concatenate([s[0, rows - 2 * WIDE :], down[:WIDE]], axis=0),
        )
        dens = jnp.concatenate([up[WIDE:], d[0, : 3 * HALF], d[0, rows - 3 * HALF :], down[WIDE:]], axis=0)
        kv = cols_of(wide, jnp.concatenate([rows_of(tall, x) for x in scal], axis=0), True)
        u = quotient(dens, kv)
        k = cols_of(wide, jnp.concatenate([rows_of(tall, x) for x in (u[: 2 * WIDE], u[2 * WIDE :])], axis=0), False)
        for p, start in enumerate((0, rows - WIDE)):
            kp = k[p * WIDE : (p + 1) * WIDE]
            outs[2 * p][...] = log_term(w[0], s[0, start : start + WIDE, LANES:-LANES], kp)
            outs[2 * p + 1][...] = kp

    out = [(WIDE, cols - 2 * LANES)] * 4
    return call(body, out, [smem()] + [vmem()] * 6, "edges", deps)(
        weights, scaling, densities, tall, wide, one, two
    )


def side_pack(scaling, densities, one, two, deps):
    rows, cols = scaling.shape[1:]
    tall = rows + 2 * WIDE
    pair = lax.axis_size("gy") == 2

    def body(s, d, one_ref, two_ref, *outs):
        lane = lax.broadcasted_iota(jnp.int32, (tall, LANES), 1)
        zero = jnp.zeros((HALF, LANES), F32)

        def tallest(which):
            up, down = halo_rows(one_ref, two_ref, which)
            scal = jnp.concatenate([up[:WIDE], s[0, :, which], down[:WIDE]], axis=0)
            dens = jnp.concatenate([zero, up[WIDE:], d[0, :, which], down[WIDE:], zero], axis=0)
            return scal, dens

        scal, dens = tallest(slice(cols - LANES, cols))
        last = jnp.where(lane >= WIDE, scal, pltpu.roll(dens, HALF, 1))
        scal, dens = tallest(slice(0, LANES))
        first = jnp.where(lane < WIDE, scal, pltpu.roll(dens, WIDE, 1))
        if pair:
            outs[0][...] = jnp.where(lax.axis_index("gy") == 0, last, first)
        else:
            outs[0][...] = last
            outs[1][...] = first

    out = [(tall, LANES)] * (1 if pair else 2)
    return call(body, out, [vmem()] * 4, "side_pack", deps)(scaling, densities, one, two)


def side_chunks(weights, scaling, densities, tall, one, two, from_left, from_right, deps):
    rows, cols = scaling.shape[1:]
    long = rows + 2 * WIDE
    width = cols - 2 * LANES
    count = rows * 2 * LANES // (WIDE * width)
    blocks = width // (2 * LANES)
    pair = lax.axis_size("gy") == 2

    def body(w, s, d, tall_ref, one_ref, two_ref, left_ref, right_ref, *outs):
        tall = pair_of(tall_ref)
        short = band(BLOCK + WIDE, BLOCK, HALF)
        here, last = lax.axis_index("gy"), lax.axis_size("gy") - 1
        left = jnp.where(here == 0, 0.0, left_ref[...])
        right = jnp.where(here == last, 0.0, right_ref[...])
        lane = lax.broadcasted_iota(jnp.int32, (long, LANES), 1)
        inner = slice(HALF, long - HALF)

        def block(which):
            up, down = halo_rows(one_ref, two_ref, which)
            scal = jnp.concatenate([up[:WIDE], s[0, :, which], down[:WIDE]], axis=0)
            dens = jnp.concatenate([up[WIDE:], d[0, :, which], down[WIDE:]], axis=0)
            return pltpu.roll(scal, WIDE, 1), dens

        def cols_of_both(sides, band):
            y = times(split(jnp.concatenate(sides, axis=0)), band)
            n = sides[0].shape[0]
            return y[:n], y[n:]

        small = lane[inner]
        (s0, d0), (s1, d1) = block(slice(0, LANES)), block(slice(LANES, 2 * LANES))
        scal = jnp.concatenate([jnp.where(lane < WIDE, pltpu.roll(left, WIDE, 1), s0), jnp.where(lane < WIDE, s0, s1)], axis=1)
        d0, d1 = pltpu.roll(d0, HALF, 1), pltpu.roll(d1, HALF, 1)
        dens = jnp.concatenate(
            [jnp.where(small < HALF, left[inner], d0), jnp.where(small < HALF, d0, d1)[:, :WIDE]], axis=1
        )
        first = scal, dens
        (s0, d0), (s1, d1) = block(slice(cols - 2 * LANES, cols - LANES)), block(slice(cols - LANES, cols))
        scal = jnp.concatenate([jnp.where(lane < WIDE, s0, s1), jnp.where(lane < WIDE, s1, pltpu.roll(right, WIDE, 1))], axis=1)
        d0, d1 = pltpu.roll(d0, HALF, 1), pltpu.roll(d1, HALF, 1)
        halo = pltpu.roll(right, LANES - HALF, 1)[inner]
        dens = jnp.concatenate(
            [jnp.where(small < HALF, d0, d1), jnp.where(small < HALF, d1, halo)[:, :WIDE]], axis=1
        )
        both = first, (scal, dens)
        kv = cols_of_both([rows_of(tall, scal) for scal, _ in both], short)
        u = [quotient(dens, x) for (_, dens), x in zip(both, kv)]
        k0, k1 = cols_of_both([rows_of(tall, x) for x in u], part(short, slice(BLOCK), slice(LANES)))
        for p in range(count):
            for b in range(blocks):
                r = slice((p * blocks + b) * WIDE, (p * blocks + b + 1) * WIDE)
                c = 2 * LANES * b
                outs[2 * p][:, c : c + LANES] = log_term(w[0], s[0, r, :LANES], k0[r])
                outs[2 * p][:, c + LANES : c + 2 * LANES] = log_term(w[0], s[0, r, cols - LANES :], k1[r])
                outs[2 * p + 1][:, c : c + LANES] = k0[r]
                outs[2 * p + 1][:, c + LANES : c + 2 * LANES] = k1[r]

    out = [(WIDE, width)] * (2 * count)
    return call(body, out, [smem()] + [vmem()] * 7, "sides", deps)(
        weights, scaling, densities, tall, one, two, from_left, from_right
    )


def add(a, b, deps, name="add"):
    def body(a_ref, b_ref, out_ref):
        out_ref[...] = a_ref[...] + b_ref[...]

    return call(body, [a.shape], [vmem()] * 2, name, deps)(a, b)[0]


def in_middle():
    z = lax.axis_index("map")
    return (z == 1) | (z == 2)


def mass_of(raw, mass_ref):
    rows, cols = raw.shape
    total = jnp.sum(raw.reshape(rows // 8, 8, cols), axis=0)
    total = sum(total[:, k : k + LANES] for k in range(0, cols, LANES))
    return total if mass_ref is None else total + mass_ref[...]


def add_and_pass(a, b, term, mass, deps):
    inputs = [a, b, term] + ([] if mass is None else [mass])
    n = len(inputs)

    def body(*refs):
        out_ref, send_ref, mass_ref = refs[n:]
        total = refs[0][...] + refs[1][...]
        out_ref[...] = total
        send_ref[...] = jnp.where(in_middle(), total, refs[2][...])
        mass_ref[...] = mass_of(jnp.exp(total), None if mass is None else refs[3])

    return call(body, [a.shape, a.shape, (8, LANES)], [vmem()] * n, "add_and_pass", deps)(*inputs)


def weigh(logs, mass, deps):
    inputs = [logs] + ([] if mass is None else [mass])
    n = len(inputs)

    def body(*refs):
        refs[n][...] = mass_of(jnp.exp(refs[0][...]), None if mass is None else refs[1])

    return call(body, [(8, LANES)], [vmem()] * n, "weigh", deps)(*inputs)


def finish(held, landed, ku, deps, name="finish"):
    inputs = [held] + ([] if landed is None else [landed]) + [ku]
    n = len(inputs)

    def body(*refs):
        raw_ref, quot_ref = refs[n:]
        logs = refs[0][...]
        if landed is not None:
            logs = jnp.where(in_middle(), logs, refs[1][...])
        raw = jnp.exp(logs)
        raw_ref[...] = raw
        quot_ref[...] = raw / refs[n - 1][...]

    return call(body, [held.shape, held.shape], [vmem()] * n, name, deps)(*inputs)


def sum_grid(mass, axes):
    for axis in axes:
        count = lax.axis_size(axis)
        if count & (count - 1):
            mass = lax.psum(mass, axis)
            continue
        step = 1
        while step < count:
            mass = mass + lax.ppermute(mass, axis, [(i, i ^ step) for i in range(count)])
            step *= 2
    return mass


def assemble(masses, places, raws, quots, rows, cols, cells):
    n, m = len(places), len(masses)

    def body(*refs):
        mass, raw, quot = refs[:m], refs[m : m + n], refs[m + n : m + 2 * n]
        bary_hbm, new_hbm, bary, new, sems = refs[m + 2 * n :]
        total = mass[0][...]
        if m > 1:
            total = jnp.where(in_middle(), total + mass[3][...], mass[2][...] + mass[1][...])
        scale = cells / jnp.sum(total)
        copies = []
        for row in range(0, rows, WIDE):
            band_rows = pl.ds(row, WIDE)
            for k, place in enumerate(places):
                for r0, c0, width, from_col in place:
                    if r0 == row:
                        piece = (slice(None), slice(from_col, from_col + width))
                        bary[row : row + WIDE, c0 : c0 + width] = raw[k][piece] * scale
                        new[row : row + WIDE, c0 : c0 + width] = quot[k][piece] * scale
            for source, target in ((bary, bary_hbm.at[band_rows]), (new, new_hbm.at[0, band_rows])):
                copies.append(pltpu.make_async_copy(source.at[band_rows], target, sems.at[len(copies)]))
                copies[-1].start()
        for copy in copies:
            copy.wait()

    tile = pltpu.VMEM((rows, cols), F32)
    return call(
        body,
        [(rows, cols), (1, rows, cols)],
        [vmem()] * (m + 2 * n),
        "assemble",
        scratch=[tile, tile, pltpu.SemaphoreType.DMA((2 * rows // WIDE,))],
        out_specs=[pl.BlockSpec(memory_space=pl.ANY)] * 2,
    )(*masses, *raws, *quots)


def chunk_places(rows, cols):
    width = cols - 2 * LANES
    starts = list(range(WIDE, rows - WIDE, WIDE)) + [0, rows - WIDE]
    places = [[(r, LANES, width, 0)] for r in starts]
    blocks = width // (2 * LANES)
    for p in range(rows * 2 * LANES // (WIDE * width)):
        place = []
        for b in range(blocks):
            r = (p * blocks + b) * WIDE
            place += [(r, 0, LANES, 2 * LANES * b), (r, cols - LANES, LANES, 2 * LANES * b + LANES)]
        places.append(place)
    return places


def local(densities, scaling, weights):
    rows, cols = scaling.shape[1:]
    places = chunk_places(rows, cols)
    n = len(places)
    gx, gy = lax.axis_size("gx"), lax.axis_size("gy")
    cells = float(rows * cols * gx * gy)
    maps = lax.axis_size("map")
    chain = [()]

    def done(*values):
        chain[0] = (values[0],)
        return values

    near = [(i, i ^ 1) for i in range(gx)]
    far = []
    for i in range(gx):
        for j in range(gy):
            other = ((i + 1) // 2 * 2 - (1 if i % 2 == 0 else 0)) if 0 < i < gx - 1 else i
            far.append((i * gy + j, other * gy + (j if other != i else j ^ 1)))
    outer = [(0, 1), (1, 0), (2, 3), (3, 2)]
    middle = []
    for g in range(gx):
        middle += [(gx + g, 2 * gx + g), (2 * gx + g, gx + g), (g, g ^ 1), (3 * gx + g, 3 * gx + (g ^ 1))]

    term, ku, sent, crossed, held, got = [None] * n, [None] * n, [None] * n, [None] * n, [None] * n, [None] * (n + LAG)
    raws, quots, mass = [None] * n, [None] * n, [None]

    def outward(k, value):
        if maps == 4 and k < n + LAG:
            got[k] = lax.ppermute(value, "map", outer)

    def receive(k):
        if maps == 4:
            (sent[k],) = done(add(term[k], got[k], chain[0]))
            crossed[k] = lax.ppermute(sent[k], ("map", "gx"), middle)

    def total(k):
        if maps == 4:
            later = term[min(k + LAG, n - 1)]
            held[k], passed, mass[0] = done(*add_and_pass(sent[k], crossed[k], later, mass[0], chain[0]))
            outward(k + LAG, passed)
        else:
            held[k] = lax.psum(term[k], "map")
            (mass[0],) = done(*weigh(held[k], mass[0], chain[0]))

    def close(k, name="finish"):
        raws[k], quots[k] = done(*finish(held[k], got[k + LAG], ku[k], chain[0], name))

    def take(first, values):
        for k in range(len(values) // 2):
            term[first + k], ku[first + k] = values[2 * k : 2 * k + 2]
        done(values[0])

    *values, tall, wide, scaling, densities, one = first_chunk(weights, scaling, densities)
    take(0, values)
    outward(0, term[0])
    one = lax.ppermute(one, "gx", near)
    *values, two = inner_chunks(weights, scaling, densities, tall, wide, (one,))
    take(1, values)
    for k in range(1, LAG):
        outward(k, term[k])
    two = lax.ppermute(two, ("gx", "gy"), far)
    receive(0)
    inner_count = rows // WIDE - 2
    receive(1)
    packs = done(*side_pack(scaling, densities, one, two, chain[0]))
    if gy == 2:
        from_left = from_right = lax.ppermute(packs[0], "gy", [(0, 1), (1, 0)])
    else:
        from_left = lax.ppermute(packs[0], "gy", [(i, i + 1) for i in range(gy - 1)])
        from_right = lax.ppermute(packs[1], "gy", [(i + 1, i) for i in range(gy - 1)])
    take(inner_count, edge_chunks(weights, scaling, densities, tall, wide, one, two, chain[0]))
    total(0)
    receive(2)
    total(1)
    receive(3)
    sides = side_chunks(weights, scaling, densities, tall, one, two, from_left, from_right, chain[0])
    take(inner_count + 2, sides)
    total(2)
    for k in range(4, n):
        receive(k)
        total(k - 1)
        close(k - LAG)
    close(n - LAG)
    total(n - 1)
    if maps == 4 and gx == 4 and gy == 2:
        own = sum_grid(mass[0], ("gx",))
        swap = [(i * gy + j, (i ^ 1) * gy + 1 - j) for i in range(4) for j in range(gy)]
        masses = [
            own,
            lax.ppermute(own, ("map", "gy"), swap),
            lax.ppermute(own, "map", outer),
            lax.ppermute(own, "gy", [(0, 1), (1, 0)]),
        ]
        for k in range(n - 3, n):
            close(k, "finish_last")
    else:
        masses = [sum_grid(mass[0], ("gx", "gy"))]
        if maps == 4:
            masses = [jnp.where(in_middle(), masses[0], lax.ppermute(masses[0], "map", outer))]
        for k in range(n - 3, n):
            close(k)
    bary, new = assemble(masses, places, raws, quots, rows, cols, cells)
    return bary, new


def solution(mesh):
    placed = (P("map", "gx", "gy"), P("map", "gx", "gy"), P("map"))
    return jax.shard_map(
        local,
        mesh=mesh,
        in_specs=placed,
        out_specs=(P("gx", "gy"), P("map", "gx", "gy")),
        check_vma=False,
    )
```

```python
import jax
import jax.numpy as jnp
import numpy as np
from jax import lax
from jax.experimental import pallas as pl
from jax.experimental.pallas import tpu as pltpu
from jax.sharding import PartitionSpec as P

HALF = 32
SIGMA = 16
WIDE = 2 * HALF
LANES = 128
BLOCK = 192
LAG = 4
F32 = jnp.float32
BF16 = jnp.bfloat16


def inverse_total():
    taps = np.arange(-HALF, HALF + 1, dtype=np.float64)
    return float(1.0 / np.exp(-taps * taps / (2.0 * SIGMA * SIGMA)).sum())


def split(x):
    high = x.astype(BF16)
    low = (x - high.astype(F32)).astype(BF16)
    return high, low


def band(rows, cols, shift):
    r = lax.broadcasted_iota(jnp.int32, (rows, cols), 0)
    c = lax.broadcasted_iota(jnp.int32, (rows, cols), 1)
    off = (r - c - shift).astype(F32)
    values = jnp.exp(off * off * (-0.5 / (SIGMA * SIGMA))) * inverse_total()
    return split(jnp.where(jnp.abs(off) <= HALF, values, 0.0))


def mm(a, b):
    return jnp.dot(a, b, preferred_element_type=F32)


def times(left, right):
    (lh, ll), (rh, rl) = left, right
    return mm(jnp.concatenate([lh, lh, ll], axis=1), jnp.concatenate([rh, rl, rh], axis=0))


def part(pair, rows=slice(None), cols=slice(None)):
    return pair[0][rows, cols], pair[1][rows, cols]


def rows_of(tall, x):
    x = split(x)
    n = x[0].shape[0] - WIDE
    out = []
    for start in range(0, n, BLOCK):
        m = min(BLOCK, n - start)
        out.append(times(part(tall, slice(m), slice(m + WIDE)), part(x, slice(start, start + m + WIDE))))
    return out[0] if len(out) == 1 else jnp.concatenate(out, axis=0)


def cols_of(wide, x, padded):
    margin = 0 if padded else LANES
    width = x.shape[1]
    x = split(x)
    out = []
    for start in range(margin, width - margin, 256):
        lo, hi = max(start - LANES, 0), min(start + 256 + LANES, width)
        rows = slice(lo - (start - LANES), hi - (start - LANES))
        out.append(times(part(x, cols=slice(lo, hi)), part(wide, rows)))
    return jnp.concatenate(out, axis=1)


def quotient(dens, kv):
    return jnp.where(dens > 0.0, dens / kv, 0.0)


def pair_of(ref):
    return ref[0], ref[1]


def log_term(weight, scal, ku):
    return weight * jnp.log(scal * ku)


def vmem():
    return pl.BlockSpec(memory_space=pltpu.VMEM)


def smem():
    return pl.BlockSpec(memory_space=pltpu.SMEM)


def hbm():
    return pl.BlockSpec(memory_space=pltpu.HBM)


COST = {'finish_last': 2.0, 'add': 4.0, 'inner': 2.5, 'edges': 2.3, 'sides': 2.5}


def call(body, out, in_specs, name, deps=(), scratch=(), out_specs=None):
    n = len(in_specs)

    def run(*refs):
        body(*refs[:n], *refs[n + len(deps) :])

    kernel = pl.pallas_call(
        run,
        out_shape=[jax.ShapeDtypeStruct(s, F32) if isinstance(s, tuple) else s for s in out],
        in_specs=list(in_specs) + [pl.BlockSpec(memory_space=pl.ANY)] * len(deps),
        out_specs=out_specs or [vmem()] * len(out),
        scratch_shapes=list(scratch),
        compiler_params=pltpu.CompilerParams(vmem_limit_bytes=40 * 1024 * 1024),
        cost_estimate=pl.CostEstimate(flops=int(COST.get(name, 0) * 1e9), bytes_accessed=0, transcendentals=0),
        name=name,
    )
    return lambda *args: kernel(*args, *deps)


def fill_pack(s, d, pack, last):
    rows = s.shape[1]
    for start, x, n in ((0, s, WIDE), (WIDE, d, HALF)):
        pack[start : start + n] = jnp.where(last, x[0, rows - n :], x[0, :n])


def first_chunk(weights, scaling, densities):
    rows, cols = scaling.shape[1:]
    tall_n, dens_n = 3 * WIDE, 2 * WIDE

    def body(w, s_hbm, d_hbm, term, ku, tall_ref, wide_ref, s, d, near, sems):
        copies = []
        for start, stop in ((0, tall_n), (tall_n, rows)):
            for source, ref in ((s_hbm, s), (d_hbm, d)):
                piece = (0, pl.ds(start, stop - start))
                copies.append(pltpu.make_async_copy(source.at[piece], ref.at[piece], sems.at[len(copies)]))
        for copy in copies[:2]:
            copy.start()
        tall = band(BLOCK, BLOCK + WIDE, -HALF)
        wide = band(512, 256, LANES)
        tall_ref[0], tall_ref[1] = tall
        wide_ref[0], wide_ref[1] = wide
        copies[0].wait()
        for copy in copies[2:]:
            copy.start()
        kv = cols_of(wide, rows_of(tall, s[0, :tall_n]), True)
        copies[1].wait()
        u = quotient(d[0, HALF : HALF + dens_n], kv)
        k = cols_of(wide, rows_of(tall, u), False)
        ku[...] = k
        term[...] = log_term(w[0], s[0, WIDE : 2 * WIDE, LANES:-LANES], k)
        for copy in copies[2:]:
            copy.wait()
        fill_pack(s, d, near, lax.rem(lax.axis_index("gx"), 2) == 0)

    inner = (WIDE, cols - 2 * LANES)
    bands = [jax.ShapeDtypeStruct((2, BLOCK, BLOCK + WIDE), BF16), jax.ShapeDtypeStruct((2, 512, 256), BF16)]
    whole, pack = (1, rows, cols), (WIDE + HALF, cols)
    out = [inner, inner, *bands, whole, whole, pack]
    return call(body, out, [smem(), hbm(), hbm()], "first", (), [pltpu.SemaphoreType.DMA((4,))])(
        weights,
        pltpu.with_memory_space_constraint(scaling, pltpu.HBM),
        pltpu.with_memory_space_constraint(densities, pltpu.HBM),
    )


def inner_chunks(weights, scaling, densities, tall, wide, deps):
    rows, cols = scaling.shape[1:]
    count = rows // WIDE - 3

    def body(w, s, d, tall_ref, wide_ref, *outs):
        tall, wide = pair_of(tall_ref), pair_of(wide_ref)
        kv = cols_of(wide, rows_of(tall, s[0, WIDE:]), True)
        u = quotient(d[0, WIDE + HALF : rows - HALF], kv)
        k = cols_of(wide, rows_of(tall, u), False)
        term = log_term(w[0], s[0, 2 * WIDE : rows - WIDE, LANES:-LANES], k)
        for p in range(count):
            outs[2 * p][...] = term[p * WIDE : (p + 1) * WIDE]
            outs[2 * p + 1][...] = k[p * WIDE : (p + 1) * WIDE]
        fill_pack(s, d, outs[2 * count], lax.rem(lax.axis_index("gx"), 2) == 1)

    out = [(WIDE, cols - 2 * LANES)] * (2 * count) + [(WIDE + HALF, cols)]
    return call(body, out, [smem()] + [vmem()] * 4, "inner", deps)(weights, scaling, densities, tall, wide)


def halo_rows(one, two, cols=slice(None)):
    here, count = lax.axis_index("gx"), lax.axis_size("gx")
    odd = lax.rem(here, 2) == 1
    near, far = one[:, cols], two[:, cols]
    far = jnp.where((here == 0) | (here == count - 1), 0.0, far)
    return jnp.where(odd, near, far), jnp.where(odd, far, near)


def edge_chunks(weights, scaling, densities, tall, wide, one, two, deps):
    rows, cols = scaling.shape[1:]

    def body(w, s, d, tall_ref, wide_ref, one_ref, two_ref, *outs):
        tall, wide = pair_of(tall_ref), pair_of(wide_ref)
        up, down = halo_rows(one_ref, two_ref)
        scal = (
            jnp.concatenate([up[:WIDE], s[0, : 2 * WIDE]], axis=0),
            jnp.concatenate([s[0, rows - 2 * WIDE :], down[:WIDE]], axis=0),
        )
        dens = jnp.concatenate([up[WIDE:], d[0, : 3 * HALF], d[0, rows - 3 * HALF :], down[WIDE:]], axis=0)
        kv = cols_of(wide, jnp.concatenate([rows_of(tall, x) for x in scal], axis=0), True)
        u = quotient(dens, kv)
        k = cols_of(wide, jnp.concatenate([rows_of(tall, x) for x in (u[: 2 * WIDE], u[2 * WIDE :])], axis=0), False)
        for p, start in enumerate((0, rows - WIDE)):
            kp = k[p * WIDE : (p + 1) * WIDE]
            outs[2 * p][...] = log_term(w[0], s[0, start : start + WIDE, LANES:-LANES], kp)
            outs[2 * p + 1][...] = kp

    out = [(WIDE, cols - 2 * LANES)] * 4
    return call(body, out, [smem()] + [vmem()] * 6, "edges", deps)(
        weights, scaling, densities, tall, wide, one, two
    )


def side_pack(scaling, densities, one, two, deps):
    rows, cols = scaling.shape[1:]
    tall = rows + 2 * WIDE
    pair = lax.axis_size("gy") == 2

    def body(s, d, one_ref, two_ref, *outs):
        lane = lax.broadcasted_iota(jnp.int32, (tall, LANES), 1)
        zero = jnp.zeros((HALF, LANES), F32)

        def tallest(which):
            up, down = halo_rows(one_ref, two_ref, which)
            scal = jnp.concatenate([up[:WIDE], s[0, :, which], down[:WIDE]], axis=0)
            dens = jnp.concatenate([zero, up[WIDE:], d[0, :, which], down[WIDE:], zero], axis=0)
            return scal, dens

        scal, dens = tallest(slice(cols - LANES, cols))
        last = jnp.where(lane >= WIDE, scal, pltpu.roll(dens, HALF, 1))
        scal, dens = tallest(slice(0, LANES))
        first = jnp.where(lane < WIDE, scal, pltpu.roll(dens, WIDE, 1))
        if pair:
            outs[0][...] = jnp.where(lax.axis_index("gy") == 0, last, first)
        else:
            outs[0][...] = last
            outs[1][...] = first

    out = [(tall, LANES)] * (1 if pair else 2)
    return call(body, out, [vmem()] * 4, "side_pack", deps)(scaling, densities, one, two)


def side_chunks(weights, scaling, densities, tall, one, two, from_left, from_right, deps):
    rows, cols = scaling.shape[1:]
    long = rows + 2 * WIDE
    width = cols - 2 * LANES
    count = rows * 2 * LANES // (WIDE * width)
    blocks = width // (2 * LANES)
    pair = lax.axis_size("gy") == 2

    def body(w, s, d, tall_ref, one_ref, two_ref, left_ref, right_ref, *outs):
        tall = pair_of(tall_ref)
        short = band(BLOCK + WIDE, BLOCK, HALF)
        here, last = lax.axis_index("gy"), lax.axis_size("gy") - 1
        left = jnp.where(here == 0, 0.0, left_ref[...])
        right = jnp.where(here == last, 0.0, right_ref[...])
        lane = lax.broadcasted_iota(jnp.int32, (long, LANES), 1)
        inner = slice(HALF, long - HALF)

        def block(which):
            up, down = halo_rows(one_ref, two_ref, which)
            scal = jnp.concatenate([up[:WIDE], s[0, :, which], down[:WIDE]], axis=0)
            dens = jnp.concatenate([up[WIDE:], d[0, :, which], down[WIDE:]], axis=0)
            return pltpu.roll(scal, WIDE, 1), dens

        def cols_of_both(sides, band):
            y = times(split(jnp.concatenate(sides, axis=0)), band)
            n = sides[0].shape[0]
            return y[:n], y[n:]

        small = lane[inner]
        (s0, d0), (s1, d1) = block(slice(0, LANES)), block(slice(LANES, 2 * LANES))
        scal = jnp.concatenate([jnp.where(lane < WIDE, pltpu.roll(left, WIDE, 1), s0), jnp.where(lane < WIDE, s0, s1)], axis=1)
        d0, d1 = pltpu.roll(d0, HALF, 1), pltpu.roll(d1, HALF, 1)
        dens = jnp.concatenate(
            [jnp.where(small < HALF, left[inner], d0), jnp.where(small < HALF, d0, d1)[:, :WIDE]], axis=1
        )
        first = scal, dens
        (s0, d0), (s1, d1) = block(slice(cols - 2 * LANES, cols - LANES)), block(slice(cols - LANES, cols))
        scal = jnp.concatenate([jnp.where(lane < WIDE, s0, s1), jnp.where(lane < WIDE, s1, pltpu.roll(right, WIDE, 1))], axis=1)
        d0, d1 = pltpu.roll(d0, HALF, 1), pltpu.roll(d1, HALF, 1)
        halo = pltpu.roll(right, LANES - HALF, 1)[inner]
        dens = jnp.concatenate(
            [jnp.where(small < HALF, d0, d1), jnp.where(small < HALF, d1, halo)[:, :WIDE]], axis=1
        )
        both = first, (scal, dens)
        kv = cols_of_both([rows_of(tall, scal) for scal, _ in both], short)
        u = [quotient(dens, x) for (_, dens), x in zip(both, kv)]
        k0, k1 = cols_of_both([rows_of(tall, x) for x in u], part(short, slice(BLOCK), slice(LANES)))
        for p in range(count):
            for b in range(blocks):
                r = slice((p * blocks + b) * WIDE, (p * blocks + b + 1) * WIDE)
                c = 2 * LANES * b
                outs[2 * p][:, c : c + LANES] = log_term(w[0], s[0, r, :LANES], k0[r])
                outs[2 * p][:, c + LANES : c + 2 * LANES] = log_term(w[0], s[0, r, cols - LANES :], k1[r])
                outs[2 * p + 1][:, c : c + LANES] = k0[r]
                outs[2 * p + 1][:, c + LANES : c + 2 * LANES] = k1[r]

    out = [(WIDE, width)] * (2 * count)
    return call(body, out, [smem()] + [vmem()] * 7, "sides", deps)(
        weights, scaling, densities, tall, one, two, from_left, from_right
    )


def add(a, b, deps, name="add"):
    def body(a_ref, b_ref, out_ref):
        out_ref[...] = a_ref[...] + b_ref[...]

    return call(body, [a.shape], [vmem()] * 2, name, deps)(a, b)[0]


def in_middle():
    z = lax.axis_index("map")
    return (z == 1) | (z == 2)


def mass_of(raw, mass_ref):
    rows, cols = raw.shape
    total = jnp.sum(raw.reshape(rows // 8, 8, cols), axis=0)
    total = sum(total[:, k : k + LANES] for k in range(0, cols, LANES))
    return total if mass_ref is None else total + mass_ref[...]


def add_and_pass(a, b, term, mass, deps):
    inputs = [a, b, term] + ([] if mass is None else [mass])
    n = len(inputs)

    def body(*refs):
        out_ref, send_ref, mass_ref = refs[n:]
        total = refs[0][...] + refs[1][...]
        out_ref[...] = total
        send_ref[...] = jnp.where(in_middle(), total, refs[2][...])
        mass_ref[...] = mass_of(jnp.exp(total), None if mass is None else refs[3])

    return call(body, [a.shape, a.shape, (8, LANES)], [vmem()] * n, "add_and_pass", deps)(*inputs)


def weigh(logs, mass, deps):
    inputs = [logs] + ([] if mass is None else [mass])
    n = len(inputs)

    def body(*refs):
        refs[n][...] = mass_of(jnp.exp(refs[0][...]), None if mass is None else refs[1])

    return call(body, [(8, LANES)], [vmem()] * n, "weigh", deps)(*inputs)


def finish(held, landed, ku, deps, name="finish"):
    inputs = [held] + ([] if landed is None else [landed]) + [ku]
    n = len(inputs)

    def body(*refs):
        raw_ref, quot_ref = refs[n:]
        logs = refs[0][...]
        if landed is not None:
            logs = jnp.where(in_middle(), logs, refs[1][...])
        raw = jnp.exp(logs)
        raw_ref[...] = raw
        quot_ref[...] = raw / refs[n - 1][...]

    return call(body, [held.shape, held.shape], [vmem()] * n, name, deps)(*inputs)


def sum_grid(mass, axes):
    for axis in axes:
        count = lax.axis_size(axis)
        if count & (count - 1):
            mass = lax.psum(mass, axis)
            continue
        step = 1
        while step < count:
            mass = mass + lax.ppermute(mass, axis, [(i, i ^ step) for i in range(count)])
            step *= 2
    return mass


def assemble(masses, places, raws, quots, rows, cols, cells):
    n, m = len(places), len(masses)

    def body(*refs):
        mass, raw, quot = refs[:m], refs[m : m + n], refs[m + n : m + 2 * n]
        bary_hbm, new_hbm, bary, new, sems = refs[m + 2 * n :]
        total = mass[0][...]
        if m > 1:
            total = jnp.where(in_middle(), total + mass[3][...], mass[2][...] + mass[1][...])
        scale = cells / jnp.sum(total)
        copies = []
        for row in range(0, rows, WIDE):
            band_rows = pl.ds(row, WIDE)
            for k, place in enumerate(places):
                for r0, c0, width, from_col in place:
                    if r0 == row:
                        piece = (slice(None), slice(from_col, from_col + width))
                        bary[row : row + WIDE, c0 : c0 + width] = raw[k][piece] * scale
                        new[row : row + WIDE, c0 : c0 + width] = quot[k][piece] * scale
            for source, target in ((bary, bary_hbm.at[band_rows]), (new, new_hbm.at[0, band_rows])):
                copies.append(pltpu.make_async_copy(source.at[band_rows], target, sems.at[len(copies)]))
                copies[-1].start()
        for copy in copies:
            copy.wait()

    tile = pltpu.VMEM((rows, cols), F32)
    return call(
        body,
        [(rows, cols), (1, rows, cols)],
        [vmem()] * (m + 2 * n),
        "assemble",
        scratch=[tile, tile, pltpu.SemaphoreType.DMA((2 * rows // WIDE,))],
        out_specs=[pl.BlockSpec(memory_space=pl.ANY)] * 2,
    )(*masses, *raws, *quots)


def chunk_places(rows, cols):
    width = cols - 2 * LANES
    starts = list(range(WIDE, rows - WIDE, WIDE)) + [0, rows - WIDE]
    places = [[(r, LANES, width, 0)] for r in starts]
    blocks = width // (2 * LANES)
    for p in range(rows * 2 * LANES // (WIDE * width)):
        place = []
        for b in range(blocks):
            r = (p * blocks + b) * WIDE
            place += [(r, 0, LANES, 2 * LANES * b), (r, cols - LANES, LANES, 2 * LANES * b + LANES)]
        places.append(place)
    return places


def local(densities, scaling, weights):
    rows, cols = scaling.shape[1:]
    places = chunk_places(rows, cols)
    n = len(places)
    gx, gy = lax.axis_size("gx"), lax.axis_size("gy")
    cells = float(rows * cols * gx * gy)
    maps = lax.axis_size("map")
    chain = [()]

    def done(*values):
        chain[0] = (values[0],)
        return values

    near = [(i, i ^ 1) for i in range(gx)]
    far = []
    for i in range(gx):
        for j in range(gy):
            other = ((i + 1) // 2 * 2 - (1 if i % 2 == 0 else 0)) if 0 < i < gx - 1 else i
            far.append((i * gy + j, other * gy + (j if other != i else j ^ 1)))
    outer = [(0, 1), (1, 0), (2, 3), (3, 2)]
    middle = []
    for g in range(gx):
        middle += [(gx + g, 2 * gx + g), (2 * gx + g, gx + g), (g, g ^ 1), (3 * gx + g, 3 * gx + (g ^ 1))]

    term, ku, sent, crossed, held, got = [None] * n, [None] * n, [None] * n, [None] * n, [None] * n, [None] * (n + LAG)
    raws, quots, mass = [None] * n, [None] * n, [None]

    def outward(k, value):
        if maps == 4 and k < n + LAG:
            got[k] = lax.ppermute(value, "map", outer)

    def receive(k):
        if maps == 4:
            (sent[k],) = done(add(term[k], got[k], chain[0]))
            crossed[k] = lax.ppermute(sent[k], ("map", "gx"), middle)

    def total(k):
        if maps == 4:
            later = term[min(k + LAG, n - 1)]
            held[k], passed, mass[0] = done(*add_and_pass(sent[k], crossed[k], later, mass[0], chain[0]))
            outward(k + LAG, passed)
        else:
            held[k] = lax.psum(term[k], "map")
            (mass[0],) = done(*weigh(held[k], mass[0], chain[0]))

    def close(k, name="finish"):
        raws[k], quots[k] = done(*finish(held[k], got[k + LAG], ku[k], chain[0], name))

    def take(first, values):
        for k in range(len(values) // 2):
            term[first + k], ku[first + k] = values[2 * k : 2 * k + 2]
        done(values[0])

    *values, tall, wide, scaling, densities, one = first_chunk(weights, scaling, densities)
    take(0, values)
    outward(0, term[0])
    one = lax.ppermute(one, "gx", near)
    *values, two = inner_chunks(weights, scaling, densities, tall, wide, (one,))
    take(1, values)
    for k in range(1, LAG):
        outward(k, term[k])
    two = lax.ppermute(two, ("gx", "gy"), far)
    receive(0)
    inner_count = rows // WIDE - 2
    receive(1)
    packs = done(*side_pack(scaling, densities, one, two, chain[0]))
    if gy == 2:
        from_left = from_right = lax.ppermute(packs[0], "gy", [(0, 1), (1, 0)])
    else:
        from_left = lax.ppermute(packs[0], "gy", [(i, i + 1) for i in range(gy - 1)])
        from_right = lax.ppermute(packs[1], "gy", [(i + 1, i) for i in range(gy - 1)])
    take(inner_count, edge_chunks(weights, scaling, densities, tall, wide, one, two, chain[0]))
    total(0)
    receive(2)
    total(1)
    receive(3)
    sides = side_chunks(weights, scaling, densities, tall, one, two, from_left, from_right, chain[0])
    take(inner_count + 2, sides)
    total(2)
    for k in range(4, n):
        receive(k)
        total(k - 1)
        close(k - LAG)
    close(n - LAG)
    total(n - 1)
    if maps == 4 and gx == 4 and gy == 2:
        own = mass[0] + lax.ppermute(mass[0], "gy", [(0, 1), (1, 0)])
        own = own + lax.ppermute(own, "gx", near)
        swap = [(i * gx + j, (i ^ 1) * gx + (j ^ 2)) for i in range(4) for j in range(gx)]
        masses = [
            own,
            lax.ppermute(own, ("map", "gx"), swap),
            lax.ppermute(own, "map", outer),
            lax.ppermute(own, "gx", [(i, i ^ 2) for i in range(gx)]),
        ]
        for k in range(n - 3, n):
            close(k, "finish_last")
    else:
        masses = [sum_grid(mass[0], ("gx", "gy"))]
        if maps == 4:
            masses = [jnp.where(in_middle(), masses[0], lax.ppermute(masses[0], "map", outer))]
        for k in range(n - 3, n):
            close(k)
    bary, new = assemble(masses, places, raws, quots, rows, cols, cells)
    return bary, new


def solution(mesh):
    placed = (P("map", "gx", "gy"), P("map", "gx", "gy"), P("map"))
    return jax.shard_map(
        local,
        mesh=mesh,
        in_specs=placed,
        out_specs=(P("gx", "gy"), P("map", "gx", "gy")),
        check_vma=False,
    )
```

```python
import jax
import jax.numpy as jnp
import numpy as np
from jax import lax
from jax.experimental import pallas as pl
from jax.experimental.pallas import tpu as pltpu
from jax.sharding import PartitionSpec as P

HALF = 32
SIGMA = 16
WIDE = 2 * HALF
LANES = 128
BLOCK = 192
LAG = 4
F32 = jnp.float32
BF16 = jnp.bfloat16


def inverse_total():
    taps = np.arange(-HALF, HALF + 1, dtype=np.float64)
    return float(1.0 / np.exp(-taps * taps / (2.0 * SIGMA * SIGMA)).sum())


def split(x):
    high = x.astype(BF16)
    low = (x - high.astype(F32)).astype(BF16)
    return high, low


def band(rows, cols, shift):
    r = lax.broadcasted_iota(jnp.int32, (rows, cols), 0)
    c = lax.broadcasted_iota(jnp.int32, (rows, cols), 1)
    off = (r - c - shift).astype(F32)
    values = jnp.exp(off * off * (-0.5 / (SIGMA * SIGMA))) * inverse_total()
    return split(jnp.where(jnp.abs(off) <= HALF, values, 0.0))


def mm(a, b):
    return jnp.dot(a, b, preferred_element_type=F32)


def times(left, right):
    (lh, ll), (rh, rl) = left, right
    return mm(jnp.concatenate([lh, lh, ll], axis=1), jnp.concatenate([rh, rl, rh], axis=0))


def part(pair, rows=slice(None), cols=slice(None)):
    return pair[0][rows, cols], pair[1][rows, cols]


def rows_of(tall, x):
    x = split(x)
    n = x[0].shape[0] - WIDE
    out = []
    for start in range(0, n, BLOCK):
        m = min(BLOCK, n - start)
        out.append(times(part(tall, slice(m), slice(m + WIDE)), part(x, slice(start, start + m + WIDE))))
    return out[0] if len(out) == 1 else jnp.concatenate(out, axis=0)


def cols_of(wide, x, padded):
    margin = 0 if padded else LANES
    width = x.shape[1]
    x = split(x)
    out = []
    for start in range(margin, width - margin, 256):
        lo, hi = max(start - LANES, 0), min(start + 256 + LANES, width)
        rows = slice(lo - (start - LANES), hi - (start - LANES))
        out.append(times(part(x, cols=slice(lo, hi)), part(wide, rows)))
    return jnp.concatenate(out, axis=1)


def quotient(dens, kv):
    return jnp.where(dens > 0.0, dens / kv, 0.0)


def pair_of(ref):
    return ref[0], ref[1]


def log_term(weight, scal, ku):
    return weight * jnp.log(scal * ku)


def vmem():
    return pl.BlockSpec(memory_space=pltpu.VMEM)


def smem():
    return pl.BlockSpec(memory_space=pltpu.SMEM)


def hbm():
    return pl.BlockSpec(memory_space=pltpu.HBM)


COST = {'finish_last': 2.0, 'add': 4.0, 'inner': 2.5, 'edges': 2.3, 'sides': 2.5}


def call(body, out, in_specs, name, deps=(), scratch=(), out_specs=None):
    n = len(in_specs)

    def run(*refs):
        body(*refs[:n], *refs[n + len(deps) :])

    kernel = pl.pallas_call(
        run,
        out_shape=[jax.ShapeDtypeStruct(s, F32) if isinstance(s, tuple) else s for s in out],
        in_specs=list(in_specs) + [pl.BlockSpec(memory_space=pl.ANY)] * len(deps),
        out_specs=out_specs or [vmem()] * len(out),
        scratch_shapes=list(scratch),
        compiler_params=pltpu.CompilerParams(vmem_limit_bytes=40 * 1024 * 1024),
        cost_estimate=pl.CostEstimate(flops=int(COST.get(name, 0) * 1e9), bytes_accessed=0, transcendentals=0),
        name=name,
    )
    return lambda *args: kernel(*args, *deps)


def fill_pack(s, d, pack, last):
    rows = s.shape[1]
    for start, x, n in ((0, s, WIDE), (WIDE, d, HALF)):
        pack[start : start + n] = jnp.where(last, x[0, rows - n :], x[0, :n])


def first_chunk(weights, scaling, densities):
    rows, cols = scaling.shape[1:]
    tall_n, dens_n = 3 * WIDE, 2 * WIDE

    def body(w, s_hbm, d_hbm, term, ku, tall_ref, wide_ref, s, d, near, sems):
        copies = []
        for start, stop in ((0, tall_n), (tall_n, rows)):
            for source, ref in ((s_hbm, s), (d_hbm, d)):
                piece = (0, pl.ds(start, stop - start))
                copies.append(pltpu.make_async_copy(source.at[piece], ref.at[piece], sems.at[len(copies)]))
        for copy in copies:
            copy.start()
        tall = band(BLOCK, BLOCK + WIDE, -HALF)
        wide = band(512, 256, LANES)
        tall_ref[0], tall_ref[1] = tall
        wide_ref[0], wide_ref[1] = wide
        copies[0].wait()
        kv = cols_of(wide, rows_of(tall, s[0, :tall_n]), True)
        copies[1].wait()
        u = quotient(d[0, HALF : HALF + dens_n], kv)
        k = cols_of(wide, rows_of(tall, u), False)
        ku[...] = k
        term[...] = log_term(w[0], s[0, WIDE : 2 * WIDE, LANES:-LANES], k)
        for copy in copies[2:]:
            copy.wait()
        fill_pack(s, d, near, lax.rem(lax.axis_index("gx"), 2) == 0)

    inner = (WIDE, cols - 2 * LANES)
    bands = [jax.ShapeDtypeStruct((2, BLOCK, BLOCK + WIDE), BF16), jax.ShapeDtypeStruct((2, 512, 256), BF16)]
    whole, pack = (1, rows, cols), (WIDE + HALF, cols)
    out = [inner, inner, *bands, whole, whole, pack]
    return call(body, out, [smem(), hbm(), hbm()], "first", (), [pltpu.SemaphoreType.DMA((4,))])(
        weights,
        pltpu.with_memory_space_constraint(scaling, pltpu.HBM),
        pltpu.with_memory_space_constraint(densities, pltpu.HBM),
    )


def inner_chunks(weights, scaling, densities, tall, wide, deps):
    rows, cols = scaling.shape[1:]
    count = rows // WIDE - 3

    def body(w, s, d, tall_ref, wide_ref, *outs):
        tall, wide = pair_of(tall_ref), pair_of(wide_ref)
        kv = cols_of(wide, rows_of(tall, s[0, WIDE:]), True)
        u = quotient(d[0, WIDE + HALF : rows - HALF], kv)
        k = cols_of(wide, rows_of(tall, u), False)
        term = log_term(w[0], s[0, 2 * WIDE : rows - WIDE, LANES:-LANES], k)
        for p in range(count):
            outs[2 * p][...] = term[p * WIDE : (p + 1) * WIDE]
            outs[2 * p + 1][...] = k[p * WIDE : (p + 1) * WIDE]
        fill_pack(s, d, outs[2 * count], lax.rem(lax.axis_index("gx"), 2) == 1)

    out = [(WIDE, cols - 2 * LANES)] * (2 * count) + [(WIDE + HALF, cols)]
    return call(body, out, [smem()] + [vmem()] * 4, "inner", deps)(weights, scaling, densities, tall, wide)


def halo_rows(one, two, cols=slice(None)):
    here, count = lax.axis_index("gx"), lax.axis_size("gx")
    odd = lax.rem(here, 2) == 1
    near, far = one[:, cols], two[:, cols]
    far = jnp.where((here == 0) | (here == count - 1), 0.0, far)
    return jnp.where(odd, near, far), jnp.where(odd, far, near)


def edge_chunks(weights, scaling, densities, tall, wide, one, two, deps):
    rows, cols = scaling.shape[1:]

    def body(w, s, d, tall_ref, wide_ref, one_ref, two_ref, *outs):
        tall, wide = pair_of(tall_ref), pair_of(wide_ref)
        up, down = halo_rows(one_ref, two_ref)
        scal = (
            jnp.concatenate([up[:WIDE], s[0, : 2 * WIDE]], axis=0),
            jnp.concatenate([s[0, rows - 2 * WIDE :], down[:WIDE]], axis=0),
        )
        dens = jnp.concatenate([up[WIDE:], d[0, : 3 * HALF], d[0, rows - 3 * HALF :], down[WIDE:]], axis=0)
        kv = cols_of(wide, jnp.concatenate([rows_of(tall, x) for x in scal], axis=0), True)
        u = quotient(dens, kv)
        k = cols_of(wide, jnp.concatenate([rows_of(tall, x) for x in (u[: 2 * WIDE], u[2 * WIDE :])], axis=0), False)
        for p, start in enumerate((0, rows - WIDE)):
            kp = k[p * WIDE : (p + 1) * WIDE]
            outs[2 * p][...] = log_term(w[0], s[0, start : start + WIDE, LANES:-LANES], kp)
            outs[2 * p + 1][...] = kp

    out = [(WIDE, cols - 2 * LANES)] * 4
    return call(body, out, [smem()] + [vmem()] * 6, "edges", deps)(
        weights, scaling, densities, tall, wide, one, two
    )


def side_pack(scaling, densities, one, two, deps):
    rows, cols = scaling.shape[1:]
    tall = rows + 2 * WIDE
    pair = lax.axis_size("gy") == 2

    def body(s, d, one_ref, two_ref, *outs):
        lane = lax.broadcasted_iota(jnp.int32, (tall, LANES), 1)
        zero = jnp.zeros((HALF, LANES), F32)

        def tallest(which):
            up, down = halo_rows(one_ref, two_ref, which)
            scal = jnp.concatenate([up[:WIDE], s[0, :, which], down[:WIDE]], axis=0)
            dens = jnp.concatenate([zero, up[WIDE:], d[0, :, which], down[WIDE:], zero], axis=0)
            return scal, dens

        scal, dens = tallest(slice(cols - LANES, cols))
        last = jnp.where(lane >= WIDE, scal, pltpu.roll(dens, HALF, 1))
        scal, dens = tallest(slice(0, LANES))
        first = jnp.where(lane < WIDE, scal, pltpu.roll(dens, WIDE, 1))
        if pair:
            outs[0][...] = jnp.where(lax.axis_index("gy") == 0, last, first)
        else:
            outs[0][...] = last
            outs[1][...] = first

    out = [(tall, LANES)] * (1 if pair else 2)
    return call(body, out, [vmem()] * 4, "side_pack", deps)(scaling, densities, one, two)


def side_chunks(weights, scaling, densities, tall, one, two, from_left, from_right, deps):
    rows, cols = scaling.shape[1:]
    long = rows + 2 * WIDE
    width = cols - 2 * LANES
    count = rows * 2 * LANES // (WIDE * width)
    blocks = width // (2 * LANES)
    pair = lax.axis_size("gy") == 2

    def body(w, s, d, tall_ref, one_ref, two_ref, left_ref, right_ref, *outs):
        tall = pair_of(tall_ref)
        short = band(BLOCK + WIDE, BLOCK, HALF)
        here, last = lax.axis_index("gy"), lax.axis_size("gy") - 1
        left = jnp.where(here == 0, 0.0, left_ref[...])
        right = jnp.where(here == last, 0.0, right_ref[...])
        lane = lax.broadcasted_iota(jnp.int32, (long, LANES), 1)
        inner = slice(HALF, long - HALF)

        def block(which):
            up, down = halo_rows(one_ref, two_ref, which)
            scal = jnp.concatenate([up[:WIDE], s[0, :, which], down[:WIDE]], axis=0)
            dens = jnp.concatenate([up[WIDE:], d[0, :, which], down[WIDE:]], axis=0)
            return pltpu.roll(scal, WIDE, 1), dens

        def cols_of_both(sides, band):
            y = times(split(jnp.concatenate(sides, axis=0)), band)
            n = sides[0].shape[0]
            return y[:n], y[n:]

        small = lane[inner]
        (s0, d0), (s1, d1) = block(slice(0, LANES)), block(slice(LANES, 2 * LANES))
        scal = jnp.concatenate([jnp.where(lane < WIDE, pltpu.roll(left, WIDE, 1), s0), jnp.where(lane < WIDE, s0, s1)], axis=1)
        d0, d1 = pltpu.roll(d0, HALF, 1), pltpu.roll(d1, HALF, 1)
        dens = jnp.concatenate(
            [jnp.where(small < HALF, left[inner], d0), jnp.where(small < HALF, d0, d1)[:, :WIDE]], axis=1
        )
        first = scal, dens
        (s0, d0), (s1, d1) = block(slice(cols - 2 * LANES, cols - LANES)), block(slice(cols - LANES, cols))
        scal = jnp.concatenate([jnp.where(lane < WIDE, s0, s1), jnp.where(lane < WIDE, s1, pltpu.roll(right, WIDE, 1))], axis=1)
        d0, d1 = pltpu.roll(d0, HALF, 1), pltpu.roll(d1, HALF, 1)
        halo = pltpu.roll(right, LANES - HALF, 1)[inner]
        dens = jnp.concatenate(
            [jnp.where(small < HALF, d0, d1), jnp.where(small < HALF, d1, halo)[:, :WIDE]], axis=1
        )
        both = first, (scal, dens)
        kv = cols_of_both([rows_of(tall, scal) for scal, _ in both], short)
        u = [quotient(dens, x) for (_, dens), x in zip(both, kv)]
        k0, k1 = cols_of_both([rows_of(tall, x) for x in u], part(short, slice(BLOCK), slice(LANES)))
        for p in range(count):
            for b in range(blocks):
                r = slice((p * blocks + b) * WIDE, (p * blocks + b + 1) * WIDE)
                c = 2 * LANES * b
                outs[2 * p][:, c : c + LANES] = log_term(w[0], s[0, r, :LANES], k0[r])
                outs[2 * p][:, c + LANES : c + 2 * LANES] = log_term(w[0], s[0, r, cols - LANES :], k1[r])
                outs[2 * p + 1][:, c : c + LANES] = k0[r]
                outs[2 * p + 1][:, c + LANES : c + 2 * LANES] = k1[r]

    out = [(WIDE, width)] * (2 * count)
    return call(body, out, [smem()] + [vmem()] * 7, "sides", deps)(
        weights, scaling, densities, tall, one, two, from_left, from_right
    )


def add(a, b, deps, name="add"):
    def body(a_ref, b_ref, out_ref):
        out_ref[...] = a_ref[...] + b_ref[...]

    return call(body, [a.shape], [vmem()] * 2, name, deps)(a, b)[0]


def in_middle():
    z = lax.axis_index("map")
    return (z == 1) | (z == 2)


def mass_of(raw, mass_ref):
    rows, cols = raw.shape
    total = jnp.sum(raw.reshape(rows // 8, 8, cols), axis=0)
    total = sum(total[:, k : k + LANES] for k in range(0, cols, LANES))
    return total if mass_ref is None else total + mass_ref[...]


def add_and_pass(a, b, term, mass, deps):
    inputs = [a, b, term] + ([] if mass is None else [mass])
    n = len(inputs)

    def body(*refs):
        out_ref, send_ref, mass_ref = refs[n:]
        total = refs[0][...] + refs[1][...]
        out_ref[...] = total
        send_ref[...] = jnp.where(in_middle(), total, refs[2][...])
        mass_ref[...] = mass_of(jnp.exp(total), None if mass is None else refs[3])

    return call(body, [a.shape, a.shape, (8, LANES)], [vmem()] * n, "add_and_pass", deps)(*inputs)


def weigh(logs, mass, deps):
    inputs = [logs] + ([] if mass is None else [mass])
    n = len(inputs)

    def body(*refs):
        refs[n][...] = mass_of(jnp.exp(refs[0][...]), None if mass is None else refs[1])

    return call(body, [(8, LANES)], [vmem()] * n, "weigh", deps)(*inputs)


def finish(held, landed, ku, deps, name="finish"):
    inputs = [held] + ([] if landed is None else [landed]) + [ku]
    n = len(inputs)

    def body(*refs):
        raw_ref, quot_ref = refs[n:]
        logs = refs[0][...]
        if landed is not None:
            logs = jnp.where(in_middle(), logs, refs[1][...])
        raw = jnp.exp(logs)
        raw_ref[...] = raw
        quot_ref[...] = raw / refs[n - 1][...]

    return call(body, [held.shape, held.shape], [vmem()] * n, name, deps)(*inputs)


def sum_grid(mass, axes):
    for axis in axes:
        count = lax.axis_size(axis)
        if count & (count - 1):
            mass = lax.psum(mass, axis)
            continue
        step = 1
        while step < count:
            mass = mass + lax.ppermute(mass, axis, [(i, i ^ step) for i in range(count)])
            step *= 2
    return mass


def assemble(masses, places, raws, quots, rows, cols, cells):
    n, m = len(places), len(masses)

    def body(*refs):
        mass, raw, quot = refs[:m], refs[m : m + n], refs[m + n : m + 2 * n]
        bary_hbm, new_hbm, bary, new, sems = refs[m + 2 * n :]
        total = mass[0][...]
        if m > 1:
            total = jnp.where(in_middle(), total + mass[3][...], mass[2][...] + mass[1][...])
        scale = cells / jnp.sum(jnp.sum(total, axis=0, keepdims=True), axis=1, keepdims=True)
        copies = []
        for row in range(0, rows, WIDE):
            band_rows = pl.ds(row, WIDE)
            for k, place in enumerate(places):
                for r0, c0, width, from_col in place:
                    if r0 == row:
                        piece = (slice(None), slice(from_col, from_col + width))
                        bary[row : row + WIDE, c0 : c0 + width] = raw[k][piece] * scale
                        new[row : row + WIDE, c0 : c0 + width] = quot[k][piece] * scale
            for source, target in ((bary, bary_hbm.at[band_rows]), (new, new_hbm.at[0, band_rows])):
                copies.append(pltpu.make_async_copy(source.at[band_rows], target, sems.at[len(copies)]))
                copies[-1].start()
        for copy in copies:
            copy.wait()

    tile = pltpu.VMEM((rows, cols), F32)
    return call(
        body,
        [(rows, cols), (1, rows, cols)],
        [vmem()] * (m + 2 * n),
        "assemble",
        scratch=[tile, tile, pltpu.SemaphoreType.DMA((2 * rows // WIDE,))],
        out_specs=[pl.BlockSpec(memory_space=pl.ANY)] * 2,
    )(*masses, *raws, *quots)


def chunk_places(rows, cols):
    width = cols - 2 * LANES
    starts = list(range(WIDE, rows - WIDE, WIDE)) + [0, rows - WIDE]
    places = [[(r, LANES, width, 0)] for r in starts]
    blocks = width // (2 * LANES)
    for p in range(rows * 2 * LANES // (WIDE * width)):
        place = []
        for b in range(blocks):
            r = (p * blocks + b) * WIDE
            place += [(r, 0, LANES, 2 * LANES * b), (r, cols - LANES, LANES, 2 * LANES * b + LANES)]
        places.append(place)
    return places


def local(densities, scaling, weights):
    rows, cols = scaling.shape[1:]
    places = chunk_places(rows, cols)
    n = len(places)
    gx, gy = lax.axis_size("gx"), lax.axis_size("gy")
    cells = float(rows * cols * gx * gy)
    maps = lax.axis_size("map")
    chain = [()]

    def done(*values):
        chain[0] = (values[0],)
        return values

    near = [(i, i ^ 1) for i in range(gx)]
    far = []
    for i in range(gx):
        for j in range(gy):
            other = ((i + 1) // 2 * 2 - (1 if i % 2 == 0 else 0)) if 0 < i < gx - 1 else i
            far.append((i * gy + j, other * gy + (j if other != i else j ^ 1)))
    outer = [(0, 1), (1, 0), (2, 3), (3, 2)]
    middle = []
    for g in range(gx):
        middle += [(gx + g, 2 * gx + g), (2 * gx + g, gx + g), (g, g ^ 1), (3 * gx + g, 3 * gx + (g ^ 1))]

    term, ku, sent, crossed, held, got = [None] * n, [None] * n, [None] * n, [None] * n, [None] * n, [None] * (n + LAG)
    raws, quots, mass = [None] * n, [None] * n, [None]

    def outward(k, value):
        if maps == 4 and k < n + LAG:
            got[k] = lax.ppermute(value, "map", outer)

    def receive(k):
        if maps == 4:
            (sent[k],) = done(add(term[k], got[k], chain[0]))
            crossed[k] = lax.ppermute(sent[k], ("map", "gx"), middle)

    def total(k):
        if maps == 4:
            later = term[min(k + LAG, n - 1)]
            held[k], passed, mass[0] = done(*add_and_pass(sent[k], crossed[k], later, mass[0], chain[0]))
            outward(k + LAG, passed)
        else:
            held[k] = lax.psum(term[k], "map")
            (mass[0],) = done(*weigh(held[k], mass[0], chain[0]))

    def close(k, name="finish"):
        raws[k], quots[k] = done(*finish(held[k], got[k + LAG], ku[k], chain[0], name))

    def take(first, values):
        for k in range(len(values) // 2):
            term[first + k], ku[first + k] = values[2 * k : 2 * k + 2]
        done(values[0])

    *values, tall, wide, scaling, densities, one = first_chunk(weights, scaling, densities)
    take(0, values)
    outward(0, term[0])
    one = lax.ppermute(one, "gx", near)
    *values, two = inner_chunks(weights, scaling, densities, tall, wide, (one,))
    take(1, values)
    for k in range(1, LAG):
        outward(k, term[k])
    two = lax.ppermute(two, ("gx", "gy"), far)
    receive(0)
    inner_count = rows // WIDE - 2
    receive(1)
    packs = done(*side_pack(scaling, densities, one, two, chain[0]))
    if gy == 2:
        from_left = from_right = lax.ppermute(packs[0], "gy", [(0, 1), (1, 0)])
    else:
        from_left = lax.ppermute(packs[0], "gy", [(i, i + 1) for i in range(gy - 1)])
        from_right = lax.ppermute(packs[1], "gy", [(i + 1, i) for i in range(gy - 1)])
    take(inner_count, edge_chunks(weights, scaling, densities, tall, wide, one, two, chain[0]))
    total(0)
    receive(2)
    total(1)
    receive(3)
    sides = side_chunks(weights, scaling, densities, tall, one, two, from_left, from_right, chain[0])
    take(inner_count + 2, sides)
    total(2)
    for k in range(4, n):
        receive(k)
        total(k - 1)
        close(k - LAG)
    close(n - LAG)
    total(n - 1)
    if maps == 4 and gx == 4 and gy == 2:
        own = mass[0] + lax.ppermute(mass[0], "gy", [(0, 1), (1, 0)])
        own = own + lax.ppermute(own, "gx", near)
        swap = [(i * gx + j, (i ^ 1) * gx + (j ^ 2)) for i in range(4) for j in range(gx)]
        masses = [
            own,
            lax.ppermute(own, ("map", "gx"), swap),
            lax.ppermute(own, "map", outer),
            lax.ppermute(own, "gx", [(i, i ^ 2) for i in range(gx)]),
        ]
        for k in range(n - 3, n):
            close(k, "finish_last")
    else:
        masses = [sum_grid(mass[0], ("gx", "gy"))]
        if maps == 4:
            masses = [jnp.where(in_middle(), masses[0], lax.ppermute(masses[0], "map", outer))]
        for k in range(n - 3, n):
            close(k)
    bary, new = assemble(masses, places, raws, quots, rows, cols, cells)
    return bary, new


def solution(mesh):
    placed = (P("map", "gx", "gy"), P("map", "gx", "gy"), P("map"))
    return jax.shard_map(
        local,
        mesh=mesh,
        in_specs=placed,
        out_specs=(P("gx", "gy"), P("map", "gx", "gy")),
        check_vma=False,
    )
```

```python
import jax
import jax.numpy as jnp
import numpy as np
from jax import lax
from jax.experimental import pallas as pl
from jax.experimental.pallas import tpu as pltpu
from jax.sharding import PartitionSpec as P

HALF = 32
SIGMA = 16
WIDE = 2 * HALF
LANES = 128
BLOCK = 192
LAG = 4
F32 = jnp.float32
BF16 = jnp.bfloat16


def inverse_total():
    taps = np.arange(-HALF, HALF + 1, dtype=np.float64)
    return float(1.0 / np.exp(-taps * taps / (2.0 * SIGMA * SIGMA)).sum())


def split(x):
    high = x.astype(BF16)
    low = (x - high.astype(F32)).astype(BF16)
    return high, low


def band(rows, cols, shift):
    r = lax.broadcasted_iota(jnp.int32, (rows, cols), 0)
    c = lax.broadcasted_iota(jnp.int32, (rows, cols), 1)
    off = (r - c - shift).astype(F32)
    values = jnp.exp(off * off * (-0.5 / (SIGMA * SIGMA))) * inverse_total()
    return split(jnp.where(jnp.abs(off) <= HALF, values, 0.0))


def mm(a, b):
    return jnp.dot(a, b, preferred_element_type=F32)


def times(left, right):
    (lh, ll), (rh, rl) = left, right
    return mm(jnp.concatenate([lh, lh, ll], axis=1), jnp.concatenate([rh, rl, rh], axis=0))


def part(pair, rows=slice(None), cols=slice(None)):
    return pair[0][rows, cols], pair[1][rows, cols]


def rows_of(tall, x):
    x = split(x)
    n = x[0].shape[0] - WIDE
    out = []
    for start in range(0, n, BLOCK):
        m = min(BLOCK, n - start)
        out.append(times(part(tall, slice(m), slice(m + WIDE)), part(x, slice(start, start + m + WIDE))))
    return out[0] if len(out) == 1 else jnp.concatenate(out, axis=0)


def cols_of(wide, x, padded):
    margin = 0 if padded else LANES
    width = x.shape[1]
    x = split(x)
    out = []
    for start in range(margin, width - margin, 256):
        lo, hi = max(start - LANES, 0), min(start + 256 + LANES, width)
        rows = slice(lo - (start - LANES), hi - (start - LANES))
        out.append(times(part(x, cols=slice(lo, hi)), part(wide, rows)))
    return jnp.concatenate(out, axis=1)


def quotient(dens, kv):
    return jnp.where(dens > 0.0, dens / kv, 0.0)


def pair_of(ref):
    return ref[0], ref[1]


def log_term(weight, scal, ku):
    return weight * jnp.log(scal * ku)


def vmem():
    return pl.BlockSpec(memory_space=pltpu.VMEM)


def smem():
    return pl.BlockSpec(memory_space=pltpu.SMEM)


def hbm():
    return pl.BlockSpec(memory_space=pltpu.HBM)


COST = {'finish_last': 2.0, 'add': 4.0, 'inner': 2.5, 'edges': 2.3, 'sides': 2.5}


def call(body, out, in_specs, name, deps=(), scratch=(), out_specs=None):
    n = len(in_specs)

    def run(*refs):
        body(*refs[:n], *refs[n + len(deps) :])

    kernel = pl.pallas_call(
        run,
        out_shape=[jax.ShapeDtypeStruct(s, F32) if isinstance(s, tuple) else s for s in out],
        in_specs=list(in_specs) + [pl.BlockSpec(memory_space=pl.ANY)] * len(deps),
        out_specs=out_specs or [vmem()] * len(out),
        scratch_shapes=list(scratch),
        compiler_params=pltpu.CompilerParams(vmem_limit_bytes=40 * 1024 * 1024),
        cost_estimate=pl.CostEstimate(flops=int(COST.get(name, 0) * 1e9), bytes_accessed=0, transcendentals=0),
        name=name,
    )
    return lambda *args: kernel(*args, *deps)


def fill_pack(s, d, pack, last):
    rows = s.shape[1]
    for start, x, n in ((0, s, WIDE), (WIDE, d, HALF)):
        pack[start : start + n] = jnp.where(last, x[0, rows - n :], x[0, :n])


def first_chunk(weights, scaling, densities):
    rows, cols = scaling.shape[1:]
    tall_n, dens_n = 3 * WIDE, 2 * WIDE

    def body(w, s_hbm, d_hbm, term, ku, tall_ref, wide_ref, s, d, near, sems):
        copies = []
        for start, stop in ((0, tall_n), (tall_n, rows)):
            for source, ref in ((s_hbm, s), (d_hbm, d)):
                piece = (0, pl.ds(start, stop - start))
                copies.append(pltpu.make_async_copy(source.at[piece], ref.at[piece], sems.at[len(copies)]))
        for copy in copies:
            copy.start()
        tall = band(BLOCK, BLOCK + WIDE, -HALF)
        wide = band(512, 256, LANES)
        tall_ref[0], tall_ref[1] = tall
        wide_ref[0], wide_ref[1] = wide
        copies[0].wait()
        kv = cols_of(wide, rows_of(tall, s[0, :tall_n]), True)
        copies[1].wait()
        u = quotient(d[0, HALF : HALF + dens_n], kv)
        k = cols_of(wide, rows_of(tall, u), False)
        ku[...] = k
        term[...] = log_term(w[0], s[0, WIDE : 2 * WIDE, LANES:-LANES], k)
        for copy in copies[2:]:
            copy.wait()
        fill_pack(s, d, near, lax.rem(lax.axis_index("gx"), 2) == 0)

    inner = (WIDE, cols - 2 * LANES)
    bands = [jax.ShapeDtypeStruct((2, BLOCK, BLOCK + WIDE), BF16), jax.ShapeDtypeStruct((2, 512, 256), BF16)]
    whole, pack = (1, rows, cols), (WIDE + HALF, cols)
    out = [inner, inner, *bands, whole, whole, pack]
    return call(body, out, [smem(), hbm(), hbm()], "first", (), [pltpu.SemaphoreType.DMA((4,))])(
        weights,
        pltpu.with_memory_space_constraint(scaling, pltpu.HBM),
        pltpu.with_memory_space_constraint(densities, pltpu.HBM),
    )


def inner_chunks(weights, scaling, densities, tall, wide, deps):
    rows, cols = scaling.shape[1:]
    count = rows // WIDE - 3

    def body(w, s, d, tall_ref, wide_ref, *outs):
        tall, wide = pair_of(tall_ref), pair_of(wide_ref)
        kv = cols_of(wide, rows_of(tall, s[0, WIDE:]), True)
        u = quotient(d[0, WIDE + HALF : rows - HALF], kv)
        k = cols_of(wide, rows_of(tall, u), False)
        term = log_term(w[0], s[0, 2 * WIDE : rows - WIDE, LANES:-LANES], k)
        for p in range(count):
            outs[2 * p][...] = term[p * WIDE : (p + 1) * WIDE]
            outs[2 * p + 1][...] = k[p * WIDE : (p + 1) * WIDE]
        fill_pack(s, d, outs[2 * count], lax.rem(lax.axis_index("gx"), 2) == 1)

    out = [(WIDE, cols - 2 * LANES)] * (2 * count) + [(WIDE + HALF, cols)]
    return call(body, out, [smem()] + [vmem()] * 4, "inner", deps)(weights, scaling, densities, tall, wide)


def halo_rows(one, two, cols=slice(None)):
    here, count = lax.axis_index("gx"), lax.axis_size("gx")
    odd = lax.rem(here, 2) == 1
    near, far = one[:, cols], two[:, cols]
    far = jnp.where((here == 0) | (here == count - 1), 0.0, far)
    return jnp.where(odd, near, far), jnp.where(odd, far, near)


def edge_chunks(weights, scaling, densities, tall, wide, one, two, deps):
    rows, cols = scaling.shape[1:]

    def body(w, s, d, tall_ref, wide_ref, one_ref, two_ref, *outs):
        tall, wide = pair_of(tall_ref), pair_of(wide_ref)
        up, down = halo_rows(one_ref, two_ref)
        scal = (
            jnp.concatenate([up[:WIDE], s[0, : 2 * WIDE]], axis=0),
            jnp.concatenate([s[0, rows - 2 * WIDE :], down[:WIDE]], axis=0),
        )
        dens = jnp.concatenate([up[WIDE:], d[0, : 3 * HALF], d[0, rows - 3 * HALF :], down[WIDE:]], axis=0)
        kv = cols_of(wide, jnp.concatenate([rows_of(tall, x) for x in scal], axis=0), True)
        u = quotient(dens, kv)
        k = cols_of(wide, jnp.concatenate([rows_of(tall, x) for x in (u[: 2 * WIDE], u[2 * WIDE :])], axis=0), False)
        for p, start in enumerate((0, rows - WIDE)):
            kp = k[p * WIDE : (p + 1) * WIDE]
            outs[2 * p][...] = log_term(w[0], s[0, start : start + WIDE, LANES:-LANES], kp)
            outs[2 * p + 1][...] = kp

    out = [(WIDE, cols - 2 * LANES)] * 4
    return call(body, out, [smem()] + [vmem()] * 6, "edges", deps)(
        weights, scaling, densities, tall, wide, one, two
    )


def side_pack(scaling, densities, one, two, deps):
    rows, cols = scaling.shape[1:]
    tall = rows + 2 * WIDE
    pair = lax.axis_size("gy") == 2

    def body(s, d, one_ref, two_ref, *outs):
        lane = lax.broadcasted_iota(jnp.int32, (tall, LANES), 1)
        zero = jnp.zeros((HALF, LANES), F32)

        def tallest(which):
            up, down = halo_rows(one_ref, two_ref, which)
            scal = jnp.concatenate([up[:WIDE], s[0, :, which], down[:WIDE]], axis=0)
            dens = jnp.concatenate([zero, up[WIDE:], d[0, :, which], down[WIDE:], zero], axis=0)
            return scal, dens

        scal, dens = tallest(slice(cols - LANES, cols))
        last = jnp.where(lane >= WIDE, scal, pltpu.roll(dens, HALF, 1))
        scal, dens = tallest(slice(0, LANES))
        first = jnp.where(lane < WIDE, scal, pltpu.roll(dens, WIDE, 1))
        if pair:
            outs[0][...] = jnp.where(lax.axis_index("gy") == 0, last, first)
        else:
            outs[0][...] = last
            outs[1][...] = first

    out = [(tall, LANES)] * (1 if pair else 2)
    return call(body, out, [vmem()] * 4, "side_pack", deps)(scaling, densities, one, two)


def side_chunks(weights, scaling, densities, tall, one, two, from_left, from_right, deps):
    rows, cols = scaling.shape[1:]
    long = rows + 2 * WIDE
    width = cols - 2 * LANES
    count = rows * 2 * LANES // (WIDE * width)
    blocks = width // (2 * LANES)
    pair = lax.axis_size("gy") == 2

    def body(w, s, d, tall_ref, one_ref, two_ref, left_ref, right_ref, *outs):
        tall = pair_of(tall_ref)
        short = band(BLOCK + WIDE, BLOCK, HALF)
        here, last = lax.axis_index("gy"), lax.axis_size("gy") - 1
        left = jnp.where(here == 0, 0.0, left_ref[...])
        right = jnp.where(here == last, 0.0, right_ref[...])
        lane = lax.broadcasted_iota(jnp.int32, (long, LANES), 1)
        inner = slice(HALF, long - HALF)

        def block(which):
            up, down = halo_rows(one_ref, two_ref, which)
            scal = jnp.concatenate([up[:WIDE], s[0, :, which], down[:WIDE]], axis=0)
            dens = jnp.concatenate([up[WIDE:], d[0, :, which], down[WIDE:]], axis=0)
            return pltpu.roll(scal, WIDE, 1), dens

        def cols_of_both(sides, band):
            y = times(split(jnp.concatenate(sides, axis=0)), band)
            n = sides[0].shape[0]
            return y[:n], y[n:]

        small = lane[inner]
        (s0, d0), (s1, d1) = block(slice(0, LANES)), block(slice(LANES, 2 * LANES))
        scal = jnp.concatenate([jnp.where(lane < WIDE, pltpu.roll(left, WIDE, 1), s0), jnp.where(lane < WIDE, s0, s1)], axis=1)
        d0, d1 = pltpu.roll(d0, HALF, 1), pltpu.roll(d1, HALF, 1)
        dens = jnp.concatenate(
            [jnp.where(small < HALF, left[inner], d0), jnp.where(small < HALF, d0, d1)[:, :WIDE]], axis=1
        )
        first = scal, dens
        (s0, d0), (s1, d1) = block(slice(cols - 2 * LANES, cols - LANES)), block(slice(cols - LANES, cols))
        scal = jnp.concatenate([jnp.where(lane < WIDE, s0, s1), jnp.where(lane < WIDE, s1, pltpu.roll(right, WIDE, 1))], axis=1)
        d0, d1 = pltpu.roll(d0, HALF, 1), pltpu.roll(d1, HALF, 1)
        halo = pltpu.roll(right, LANES - HALF, 1)[inner]
        dens = jnp.concatenate(
            [jnp.where(small < HALF, d0, d1), jnp.where(small < HALF, d1, halo)[:, :WIDE]], axis=1
        )
        both = first, (scal, dens)
        kv = cols_of_both([rows_of(tall, scal) for scal, _ in both], short)
        u = [quotient(dens, x) for (_, dens), x in zip(both, kv)]
        k0, k1 = cols_of_both([rows_of(tall, x) for x in u], part(short, slice(BLOCK), slice(LANES)))
        for p in range(count):
            for b in range(blocks):
                r = slice((p * blocks + b) * WIDE, (p * blocks + b + 1) * WIDE)
                c = 2 * LANES * b
                outs[2 * p][:, c : c + LANES] = log_term(w[0], s[0, r, :LANES], k0[r])
                outs[2 * p][:, c + LANES : c + 2 * LANES] = log_term(w[0], s[0, r, cols - LANES :], k1[r])
                outs[2 * p + 1][:, c : c + LANES] = k0[r]
                outs[2 * p + 1][:, c + LANES : c + 2 * LANES] = k1[r]

    out = [(WIDE, width)] * (2 * count)
    return call(body, out, [smem()] + [vmem()] * 7, "sides", deps)(
        weights, scaling, densities, tall, one, two, from_left, from_right
    )


def add(a, b, deps, name="add"):
    def body(a_ref, b_ref, out_ref):
        out_ref[...] = a_ref[...] + b_ref[...]

    return call(body, [a.shape], [vmem()] * 2, name, deps)(a, b)[0]


def in_middle():
    z = lax.axis_index("map")
    return (z == 1) | (z == 2)


def mass_of(raw, mass_ref):
    rows, cols = raw.shape
    total = jnp.sum(raw.reshape(rows // 8, 8, cols), axis=0)
    total = sum(total[:, k : k + LANES] for k in range(0, cols, LANES))
    return total if mass_ref is None else total + mass_ref[...]


def add_and_pass(a, b, term, mass, deps):
    inputs = [a, b, term] + ([] if mass is None else [mass])
    n = len(inputs)

    def body(*refs):
        out_ref, send_ref, mass_ref = refs[n:]
        total = refs[0][...] + refs[1][...]
        out_ref[...] = total
        send_ref[...] = jnp.where(in_middle(), total, refs[2][...])
        mass_ref[...] = mass_of(jnp.exp(total), None if mass is None else refs[3])

    return call(body, [a.shape, a.shape, (8, LANES)], [vmem()] * n, "add_and_pass", deps)(*inputs)


def weigh(logs, mass, deps):
    inputs = [logs] + ([] if mass is None else [mass])
    n = len(inputs)

    def body(*refs):
        refs[n][...] = mass_of(jnp.exp(refs[0][...]), None if mass is None else refs[1])

    return call(body, [(8, LANES)], [vmem()] * n, "weigh", deps)(*inputs)


def finish(held, landed, ku, deps, name="finish"):
    inputs = [held] + ([] if landed is None else [landed]) + [ku]
    n = len(inputs)

    def body(*refs):
        raw_ref, quot_ref = refs[n:]
        logs = refs[0][...]
        if landed is not None:
            logs = jnp.where(in_middle(), logs, refs[1][...])
        raw = jnp.exp(logs)
        raw_ref[...] = raw
        quot_ref[...] = raw / refs[n - 1][...]

    return call(body, [held.shape, held.shape], [vmem()] * n, name, deps)(*inputs)


def sum_grid(mass, axes):
    for axis in axes:
        count = lax.axis_size(axis)
        if count & (count - 1):
            mass = lax.psum(mass, axis)
            continue
        step = 1
        while step < count:
            mass = mass + lax.ppermute(mass, axis, [(i, i ^ step) for i in range(count)])
            step *= 2
    return mass


def assemble(masses, places, raws, quots, rows, cols, cells):
    n, m = len(places), len(masses)

    def body(*refs):
        mass, raw, quot = refs[:m], refs[m : m + n], refs[m + n : m + 2 * n]
        bary_hbm, new_hbm, bary, new, sems = refs[m + 2 * n :]
        total = mass[0][...]
        if m > 1:
            total = jnp.where(in_middle(), total + mass[3][...], mass[2][...] + mass[1][...])
        scale = cells / jnp.sum(jnp.sum(total, axis=0, keepdims=True), axis=1, keepdims=True)
        copies = []
        for row in range(0, rows, WIDE):
            band_rows = pl.ds(row, WIDE)
            for k, place in enumerate(places):
                for r0, c0, width, from_col in place:
                    if r0 == row:
                        piece = (slice(None), slice(from_col, from_col + width))
                        bary[row : row + WIDE, c0 : c0 + width] = raw[k][piece] * scale
                        new[row : row + WIDE, c0 : c0 + width] = quot[k][piece] * scale
            for source, target in ((bary, bary_hbm.at[band_rows]), (new, new_hbm.at[0, band_rows])):
                copies.append(pltpu.make_async_copy(source.at[band_rows], target, sems.at[len(copies)]))
                copies[-1].start()
        for copy in copies:
            copy.wait()

    tile = pltpu.VMEM((rows, cols), F32)
    return call(
        body,
        [(rows, cols), (1, rows, cols)],
        [vmem()] * (m + 2 * n),
        "assemble",
        scratch=[tile, tile, pltpu.SemaphoreType.DMA((2 * rows // WIDE,))],
        out_specs=[pl.BlockSpec(memory_space=pl.ANY)] * 2,
    )(*masses, *raws, *quots)


def chunk_places(rows, cols):
    width = cols - 2 * LANES
    starts = list(range(WIDE, rows - WIDE, WIDE)) + [0, rows - WIDE]
    places = [[(r, LANES, width, 0)] for r in starts]
    blocks = width // (2 * LANES)
    for p in range(rows * 2 * LANES // (WIDE * width)):
        place = []
        for b in range(blocks):
            r = (p * blocks + b) * WIDE
            place += [(r, 0, LANES, 2 * LANES * b), (r, cols - LANES, LANES, 2 * LANES * b + LANES)]
        places.append(place)
    return places


def local(densities, scaling, weights):
    rows, cols = scaling.shape[1:]
    places = chunk_places(rows, cols)
    n = len(places)
    gx, gy = lax.axis_size("gx"), lax.axis_size("gy")
    cells = float(rows * cols * gx * gy)
    maps = lax.axis_size("map")
    chain = [()]

    def done(*values):
        chain[0] = (values[0],)
        return values

    near = [(i, i ^ 1) for i in range(gx)]
    far = []
    for i in range(gx):
        for j in range(gy):
            other = ((i + 1) // 2 * 2 - (1 if i % 2 == 0 else 0)) if 0 < i < gx - 1 else i
            far.append((i * gy + j, other * gy + (j if other != i else j ^ 1)))
    outer = [(0, 1), (1, 0), (2, 3), (3, 2)]
    middle = []
    for g in range(gx):
        middle += [(gx + g, 2 * gx + g), (2 * gx + g, gx + g), (g, g ^ 1), (3 * gx + g, 3 * gx + (g ^ 1))]

    term, ku, sent, crossed, held, got = [None] * n, [None] * n, [None] * n, [None] * n, [None] * n, [None] * (n + LAG)
    raws, quots, mass = [None] * n, [None] * n, [None]

    def outward(k, value):
        if maps == 4 and k < n + LAG:
            got[k] = lax.ppermute(value, "map", outer)

    def receive(k):
        if maps == 4:
            (sent[k],) = done(add(term[k], got[k], chain[0]))
            crossed[k] = lax.ppermute(sent[k], ("map", "gx"), middle)

    def total(k):
        if maps == 4:
            later = term[min(k + LAG, n - 1)]
            held[k], passed, mass[0] = done(*add_and_pass(sent[k], crossed[k], later, mass[0], chain[0]))
            outward(k + LAG, passed)
        else:
            held[k] = lax.psum(term[k], "map")
            (mass[0],) = done(*weigh(held[k], mass[0], chain[0]))

    def close(k, name="finish"):
        raws[k], quots[k] = done(*finish(held[k], got[k + LAG], ku[k], chain[0], name))

    def take(first, values):
        for k in range(len(values) // 2):
            term[first + k], ku[first + k] = values[2 * k : 2 * k + 2]
        done(values[0])

    *values, tall, wide, scaling, densities, one = first_chunk(weights, scaling, densities)
    take(0, values)
    outward(0, term[0])
    one = lax.ppermute(one, "gx", near)
    *values, two = inner_chunks(weights, scaling, densities, tall, wide, (one,))
    take(1, values)
    for k in range(1, LAG):
        outward(k, term[k])
    two = lax.ppermute(two, ("gx", "gy"), far)
    receive(0)
    inner_count = rows // WIDE - 2
    receive(1)
    take(inner_count, edge_chunks(weights, scaling, densities, tall, wide, one, two, chain[0]))
    total(0)
    packs = done(*side_pack(scaling, densities, one, two, chain[0]))
    if gy == 2:
        from_left = from_right = lax.ppermute(packs[0], "gy", [(0, 1), (1, 0)])
    else:
        from_left = lax.ppermute(packs[0], "gy", [(i, i + 1) for i in range(gy - 1)])
        from_right = lax.ppermute(packs[1], "gy", [(i + 1, i) for i in range(gy - 1)])
    receive(2)
    total(1)
    receive(3)
    sides = side_chunks(weights, scaling, densities, tall, one, two, from_left, from_right, chain[0])
    take(inner_count + 2, sides)
    total(2)
    for k in range(4, n):
        receive(k)
        total(k - 1)
        close(k - LAG)
    close(n - LAG)
    total(n - 1)
    if maps == 4 and gx == 4 and gy == 2:
        own = mass[0] + lax.ppermute(mass[0], "gy", [(0, 1), (1, 0)])
        own = own + lax.ppermute(own, "gx", near)
        swap = [(i * gx + j, (i ^ 1) * gx + (j ^ 2)) for i in range(4) for j in range(gx)]
        masses = [
            own,
            lax.ppermute(own, ("map", "gx"), swap),
            lax.ppermute(own, "map", outer),
            lax.ppermute(own, "gx", [(i, i ^ 2) for i in range(gx)]),
        ]
        for k in range(n - 3, n):
            close(k, "finish_last")
    else:
        masses = [sum_grid(mass[0], ("gx", "gy"))]
        if maps == 4:
            masses = [jnp.where(in_middle(), masses[0], lax.ppermute(masses[0], "map", outer))]
        for k in range(n - 3, n):
            close(k)
    bary, new = assemble(masses, places, raws, quots, rows, cols, cells)
    return bary, new


def solution(mesh):
    placed = (P("map", "gx", "gy"), P("map", "gx", "gy"), P("map"))
    return jax.shard_map(
        local,
        mesh=mesh,
        in_specs=placed,
        out_specs=(P("gx", "gy"), P("map", "gx", "gy")),
        check_vma=False,
    )
```

```python
import jax
import jax.numpy as jnp
import numpy as np
from jax import lax
from jax.experimental import pallas as pl
from jax.experimental.pallas import tpu as pltpu
from jax.sharding import PartitionSpec as P

HALF = 32
SIGMA = 16
WIDE = 2 * HALF
LANES = 128
BLOCK = 192
LAG = 4
F32 = jnp.float32
BF16 = jnp.bfloat16


def inverse_total():
    taps = np.arange(-HALF, HALF + 1, dtype=np.float64)
    return float(1.0 / np.exp(-taps * taps / (2.0 * SIGMA * SIGMA)).sum())


def split(x):
    high = x.astype(BF16)
    low = (x - high.astype(F32)).astype(BF16)
    return high, low


def band(rows, cols, shift):
    r = lax.broadcasted_iota(jnp.int32, (rows, cols), 0)
    c = lax.broadcasted_iota(jnp.int32, (rows, cols), 1)
    off = (r - c - shift).astype(F32)
    values = jnp.exp(off * off * (-0.5 / (SIGMA * SIGMA))) * inverse_total()
    return split(jnp.where(jnp.abs(off) <= HALF, values, 0.0))


def mm(a, b):
    return jnp.dot(a, b, preferred_element_type=F32)


def times(left, right):
    (lh, ll), (rh, rl) = left, right
    n = lh.shape[0]
    both = mm(jnp.concatenate([lh, ll], axis=0), rh)
    return both[:n] + both[n:] + mm(lh, rl)


def part(pair, rows=slice(None), cols=slice(None)):
    return pair[0][rows, cols], pair[1][rows, cols]


def rows_of(tall, x):
    x = split(x)
    n = x[0].shape[0] - WIDE
    out = []
    for start in range(0, n, BLOCK):
        m = min(BLOCK, n - start)
        out.append(times(part(tall, slice(m), slice(m + WIDE)), part(x, slice(start, start + m + WIDE))))
    return out[0] if len(out) == 1 else jnp.concatenate(out, axis=0)


def cols_of(wide, x, padded):
    margin = 0 if padded else LANES
    width = x.shape[1]
    x = split(x)
    out = []
    for start in range(margin, width - margin, 256):
        lo, hi = max(start - LANES, 0), min(start + 256 + LANES, width)
        rows = slice(lo - (start - LANES), hi - (start - LANES))
        out.append(times(part(x, cols=slice(lo, hi)), part(wide, rows)))
    return jnp.concatenate(out, axis=1)


def quotient(dens, kv):
    return jnp.where(dens > 0.0, dens / kv, 0.0)


def pair_of(ref):
    return ref[0], ref[1]


def log_term(weight, scal, ku):
    return weight * jnp.log(scal * ku)


def vmem():
    return pl.BlockSpec(memory_space=pltpu.VMEM)


def smem():
    return pl.BlockSpec(memory_space=pltpu.SMEM)


def hbm():
    return pl.BlockSpec(memory_space=pltpu.HBM)


COST = {'finish_last': 2.0, 'add': 4.0, 'inner': 2.5, 'edges': 2.3, 'sides': 2.5}


def call(body, out, in_specs, name, deps=(), scratch=(), out_specs=None):
    n = len(in_specs)

    def run(*refs):
        body(*refs[:n], *refs[n + len(deps) :])

    kernel = pl.pallas_call(
        run,
        out_shape=[jax.ShapeDtypeStruct(s, F32) if isinstance(s, tuple) else s for s in out],
        in_specs=list(in_specs) + [pl.BlockSpec(memory_space=pl.ANY)] * len(deps),
        out_specs=out_specs or [vmem()] * len(out),
        scratch_shapes=list(scratch),
        compiler_params=pltpu.CompilerParams(vmem_limit_bytes=40 * 1024 * 1024),
        cost_estimate=pl.CostEstimate(flops=int(COST.get(name, 0) * 1e9), bytes_accessed=0, transcendentals=0),
        name=name,
    )
    return lambda *args: kernel(*args, *deps)


def fill_pack(s, d, pack, last):
    rows = s.shape[1]
    for start, x, n in ((0, s, WIDE), (WIDE, d, HALF)):
        pack[start : start + n] = jnp.where(last, x[0, rows - n :], x[0, :n])


def first_chunk(weights, scaling, densities):
    rows, cols = scaling.shape[1:]
    tall_n, dens_n = 3 * WIDE, 2 * WIDE

    def body(w, s_hbm, d_hbm, term, ku, tall_ref, wide_ref, s, d, near, sems):
        copies = []
        for start, stop in ((0, tall_n), (tall_n, rows)):
            for source, ref in ((s_hbm, s), (d_hbm, d)):
                piece = (0, pl.ds(start, stop - start))
                copies.append(pltpu.make_async_copy(source.at[piece], ref.at[piece], sems.at[len(copies)]))
        for copy in copies[:2]:
            copy.start()
        tall = band(BLOCK, BLOCK + WIDE, -HALF)
        wide = band(512, 256, LANES)
        tall_ref[0], tall_ref[1] = tall
        wide_ref[0], wide_ref[1] = wide
        copies[0].wait()
        for copy in copies[2:]:
            copy.start()
        kv = cols_of(wide, rows_of(tall, s[0, :tall_n]), True)
        copies[1].wait()
        u = quotient(d[0, HALF : HALF + dens_n], kv)
        k = cols_of(wide, rows_of(tall, u), False)
        ku[...] = k
        term[...] = log_term(w[0], s[0, WIDE : 2 * WIDE, LANES:-LANES], k)
        for copy in copies[2:]:
            copy.wait()
        fill_pack(s, d, near, lax.rem(lax.axis_index("gx"), 2) == 0)

    inner = (WIDE, cols - 2 * LANES)
    bands = [jax.ShapeDtypeStruct((2, BLOCK, BLOCK + WIDE), BF16), jax.ShapeDtypeStruct((2, 512, 256), BF16)]
    whole, pack = (1, rows, cols), (WIDE + HALF, cols)
    out = [inner, inner, *bands, whole, whole, pack]
    return call(body, out, [smem(), hbm(), hbm()], "first", (), [pltpu.SemaphoreType.DMA((4,))])(
        weights,
        pltpu.with_memory_space_constraint(scaling, pltpu.HBM),
        pltpu.with_memory_space_constraint(densities, pltpu.HBM),
    )


def inner_chunks(weights, scaling, densities, tall, wide, deps):
    rows, cols = scaling.shape[1:]
    count = rows // WIDE - 3

    def body(w, s, d, tall_ref, wide_ref, *outs):
        tall, wide = pair_of(tall_ref), pair_of(wide_ref)
        kv = cols_of(wide, rows_of(tall, s[0, WIDE:]), True)
        u = quotient(d[0, WIDE + HALF : rows - HALF], kv)
        k = cols_of(wide, rows_of(tall, u), False)
        term = log_term(w[0], s[0, 2 * WIDE : rows - WIDE, LANES:-LANES], k)
        for p in range(count):
            outs[2 * p][...] = term[p * WIDE : (p + 1) * WIDE]
            outs[2 * p + 1][...] = k[p * WIDE : (p + 1) * WIDE]
        fill_pack(s, d, outs[2 * count], lax.rem(lax.axis_index("gx"), 2) == 1)

    out = [(WIDE, cols - 2 * LANES)] * (2 * count) + [(WIDE + HALF, cols)]
    return call(body, out, [smem()] + [vmem()] * 4, "inner", deps)(weights, scaling, densities, tall, wide)


def halo_rows(one, two, cols=slice(None)):
    here, count = lax.axis_index("gx"), lax.axis_size("gx")
    odd = lax.rem(here, 2) == 1
    near, far = one[:, cols], two[:, cols]
    far = jnp.where((here == 0) | (here == count - 1), 0.0, far)
    return jnp.where(odd, near, far), jnp.where(odd, far, near)


def edge_chunks(weights, scaling, densities, tall, wide, one, two, deps):
    rows, cols = scaling.shape[1:]

    def body(w, s, d, tall_ref, wide_ref, one_ref, two_ref, *outs):
        tall, wide = pair_of(tall_ref), pair_of(wide_ref)
        up, down = halo_rows(one_ref, two_ref)
        scal = (
            jnp.concatenate([up[:WIDE], s[0, : 2 * WIDE]], axis=0),
            jnp.concatenate([s[0, rows - 2 * WIDE :], down[:WIDE]], axis=0),
        )
        dens = jnp.concatenate([up[WIDE:], d[0, : 3 * HALF], d[0, rows - 3 * HALF :], down[WIDE:]], axis=0)
        kv = cols_of(wide, jnp.concatenate([rows_of(tall, x) for x in scal], axis=0), True)
        u = quotient(dens, kv)
        k = cols_of(wide, jnp.concatenate([rows_of(tall, x) for x in (u[: 2 * WIDE], u[2 * WIDE :])], axis=0), False)
        for p, start in enumerate((0, rows - WIDE)):
            kp = k[p * WIDE : (p + 1) * WIDE]
            outs[2 * p][...] = log_term(w[0], s[0, start : start + WIDE, LANES:-LANES], kp)
            outs[2 * p + 1][...] = kp

    out = [(WIDE, cols - 2 * LANES)] * 4
    return call(body, out, [smem()] + [vmem()] * 6, "edges", deps)(
        weights, scaling, densities, tall, wide, one, two
    )


def side_pack(scaling, densities, one, two, deps):
    rows, cols = scaling.shape[1:]
    tall = rows + 2 * WIDE
    pair = lax.axis_size("gy") == 2

    def body(s, d, one_ref, two_ref, *outs):
        lane = lax.broadcasted_iota(jnp.int32, (tall, LANES), 1)
        zero = jnp.zeros((HALF, LANES), F32)

        def tallest(which):
            up, down = halo_rows(one_ref, two_ref, which)
            scal = jnp.concatenate([up[:WIDE], s[0, :, which], down[:WIDE]], axis=0)
            dens = jnp.concatenate([zero, up[WIDE:], d[0, :, which], down[WIDE:], zero], axis=0)
            return scal, dens

        scal, dens = tallest(slice(cols - LANES, cols))
        last = jnp.where(lane >= WIDE, scal, pltpu.roll(dens, HALF, 1))
        scal, dens = tallest(slice(0, LANES))
        first = jnp.where(lane < WIDE, scal, pltpu.roll(dens, WIDE, 1))
        if pair:
            outs[0][...] = jnp.where(lax.axis_index("gy") == 0, last, first)
        else:
            outs[0][...] = last
            outs[1][...] = first

    out = [(tall, LANES)] * (1 if pair else 2)
    return call(body, out, [vmem()] * 4, "side_pack", deps)(scaling, densities, one, two)


def side_chunks(weights, scaling, densities, tall, one, two, from_left, from_right, deps):
    rows, cols = scaling.shape[1:]
    long = rows + 2 * WIDE
    width = cols - 2 * LANES
    count = rows * 2 * LANES // (WIDE * width)
    blocks = width // (2 * LANES)
    pair = lax.axis_size("gy") == 2

    def body(w, s, d, tall_ref, one_ref, two_ref, left_ref, right_ref, *outs):
        tall = pair_of(tall_ref)
        short = band(BLOCK + WIDE, BLOCK, HALF)
        here, last = lax.axis_index("gy"), lax.axis_size("gy") - 1
        left = jnp.where(here == 0, 0.0, left_ref[...])
        right = jnp.where(here == last, 0.0, right_ref[...])
        lane = lax.broadcasted_iota(jnp.int32, (long, LANES), 1)
        inner = slice(HALF, long - HALF)

        def block(which):
            up, down = halo_rows(one_ref, two_ref, which)
            scal = jnp.concatenate([up[:WIDE], s[0, :, which], down[:WIDE]], axis=0)
            dens = jnp.concatenate([up[WIDE:], d[0, :, which], down[WIDE:]], axis=0)
            return pltpu.roll(scal, WIDE, 1), dens

        def cols_of_both(sides, band):
            y = times(split(jnp.concatenate(sides, axis=0)), band)
            n = sides[0].shape[0]
            return y[:n], y[n:]

        small = lane[inner]
        (s0, d0), (s1, d1) = block(slice(0, LANES)), block(slice(LANES, 2 * LANES))
        scal = jnp.concatenate([jnp.where(lane < WIDE, pltpu.roll(left, WIDE, 1), s0), jnp.where(lane < WIDE, s0, s1)], axis=1)
        d0, d1 = pltpu.roll(d0, HALF, 1), pltpu.roll(d1, HALF, 1)
        dens = jnp.concatenate(
            [jnp.where(small < HALF, left[inner], d0), jnp.where(small < HALF, d0, d1)[:, :WIDE]], axis=1
        )
        first = scal, dens
        (s0, d0), (s1, d1) = block(slice(cols - 2 * LANES, cols - LANES)), block(slice(cols - LANES, cols))
        scal = jnp.concatenate([jnp.where(lane < WIDE, s0, s1), jnp.where(lane < WIDE, s1, pltpu.roll(right, WIDE, 1))], axis=1)
        d0, d1 = pltpu.roll(d0, HALF, 1), pltpu.roll(d1, HALF, 1)
        halo = pltpu.roll(right, LANES - HALF, 1)[inner]
        dens = jnp.concatenate(
            [jnp.where(small < HALF, d0, d1), jnp.where(small < HALF, d1, halo)[:, :WIDE]], axis=1
        )
        both = first, (scal, dens)
        kv = cols_of_both([rows_of(tall, scal) for scal, _ in both], short)
        u = [quotient(dens, x) for (_, dens), x in zip(both, kv)]
        k0, k1 = cols_of_both([rows_of(tall, x) for x in u], part(short, slice(BLOCK), slice(LANES)))
        for p in range(count):
            for b in range(blocks):
                r = slice((p * blocks + b) * WIDE, (p * blocks + b + 1) * WIDE)
                c = 2 * LANES * b
                outs[2 * p][:, c : c + LANES] = log_term(w[0], s[0, r, :LANES], k0[r])
                outs[2 * p][:, c + LANES : c + 2 * LANES] = log_term(w[0], s[0, r, cols - LANES :], k1[r])
                outs[2 * p + 1][:, c : c + LANES] = k0[r]
                outs[2 * p + 1][:, c + LANES : c + 2 * LANES] = k1[r]

    out = [(WIDE, width)] * (2 * count)
    return call(body, out, [smem()] + [vmem()] * 7, "sides", deps)(
        weights, scaling, densities, tall, one, two, from_left, from_right
    )


def add(a, b, deps, name="add"):
    def body(a_ref, b_ref, out_ref):
        out_ref[...] = a_ref[...] + b_ref[...]

    return call(body, [a.shape], [vmem()] * 2, name, deps)(a, b)[0]


def in_middle():
    z = lax.axis_index("map")
    return (z == 1) | (z == 2)


def mass_of(raw, mass_ref):
    rows, cols = raw.shape
    total = jnp.sum(raw.reshape(rows // 8, 8, cols), axis=0)
    total = sum(total[:, k : k + LANES] for k in range(0, cols, LANES))
    return total if mass_ref is None else total + mass_ref[...]


def add_and_pass(a, b, term, mass, deps):
    inputs = [a, b, term] + ([] if mass is None else [mass])
    n = len(inputs)

    def body(*refs):
        out_ref, send_ref, mass_ref = refs[n:]
        total = refs[0][...] + refs[1][...]
        out_ref[...] = total
        send_ref[...] = jnp.where(in_middle(), total, refs[2][...])
        mass_ref[...] = mass_of(jnp.exp(total), None if mass is None else refs[3])

    return call(body, [a.shape, a.shape, (8, LANES)], [vmem()] * n, "add_and_pass", deps)(*inputs)


def weigh(logs, mass, deps):
    inputs = [logs] + ([] if mass is None else [mass])
    n = len(inputs)

    def body(*refs):
        refs[n][...] = mass_of(jnp.exp(refs[0][...]), None if mass is None else refs[1])

    return call(body, [(8, LANES)], [vmem()] * n, "weigh", deps)(*inputs)


def finish(held, landed, ku, deps, name="finish"):
    inputs = [held] + ([] if landed is None else [landed]) + [ku]
    n = len(inputs)

    def body(*refs):
        raw_ref, quot_ref = refs[n:]
        logs = refs[0][...]
        if landed is not None:
            logs = jnp.where(in_middle(), logs, refs[1][...])
        raw = jnp.exp(logs)
        raw_ref[...] = raw
        quot_ref[...] = raw / refs[n - 1][...]

    return call(body, [held.shape, held.shape], [vmem()] * n, name, deps)(*inputs)


def sum_grid(mass, axes):
    for axis in axes:
        count = lax.axis_size(axis)
        if count & (count - 1):
            mass = lax.psum(mass, axis)
            continue
        step = 1
        while step < count:
            mass = mass + lax.ppermute(mass, axis, [(i, i ^ step) for i in range(count)])
            step *= 2
    return mass


def assemble(masses, places, raws, quots, rows, cols, cells):
    n, m = len(places), len(masses)

    def body(*refs):
        mass, raw, quot = refs[:m], refs[m : m + n], refs[m + n : m + 2 * n]
        bary_hbm, new_hbm, bary, new, sems = refs[m + 2 * n :]
        total = mass[0][...]
        if m > 1:
            total = jnp.where(in_middle(), total + mass[3][...], mass[2][...] + mass[1][...])
        scale = cells / jnp.sum(jnp.sum(total, axis=0, keepdims=True), axis=1, keepdims=True)
        copies = []
        for row in range(0, rows, WIDE):
            band_rows = pl.ds(row, WIDE)
            for k, place in enumerate(places):
                for r0, c0, width, from_col in place:
                    if r0 == row:
                        piece = (slice(None), slice(from_col, from_col + width))
                        bary[row : row + WIDE, c0 : c0 + width] = raw[k][piece] * scale
                        new[row : row + WIDE, c0 : c0 + width] = quot[k][piece] * scale
            for source, target in ((bary, bary_hbm.at[band_rows]), (new, new_hbm.at[0, band_rows])):
                copies.append(pltpu.make_async_copy(source.at[band_rows], target, sems.at[len(copies)]))
                copies[-1].start()
        for copy in copies:
            copy.wait()

    tile = pltpu.VMEM((rows, cols), F32)
    return call(
        body,
        [(rows, cols), (1, rows, cols)],
        [vmem()] * (m + 2 * n),
        "assemble",
        scratch=[tile, tile, pltpu.SemaphoreType.DMA((2 * rows // WIDE,))],
        out_specs=[pl.BlockSpec(memory_space=pl.ANY)] * 2,
    )(*masses, *raws, *quots)


def chunk_places(rows, cols):
    width = cols - 2 * LANES
    starts = list(range(WIDE, rows - WIDE, WIDE)) + [0, rows - WIDE]
    places = [[(r, LANES, width, 0)] for r in starts]
    blocks = width // (2 * LANES)
    for p in range(rows * 2 * LANES // (WIDE * width)):
        place = []
        for b in range(blocks):
            r = (p * blocks + b) * WIDE
            place += [(r, 0, LANES, 2 * LANES * b), (r, cols - LANES, LANES, 2 * LANES * b + LANES)]
        places.append(place)
    return places


def local(densities, scaling, weights):
    rows, cols = scaling.shape[1:]
    places = chunk_places(rows, cols)
    n = len(places)
    gx, gy = lax.axis_size("gx"), lax.axis_size("gy")
    cells = float(rows * cols * gx * gy)
    maps = lax.axis_size("map")
    chain = [()]

    def done(*values):
        chain[0] = (values[0],)
        return values

    near = [(i, i ^ 1) for i in range(gx)]
    far = []
    for i in range(gx):
        for j in range(gy):
            other = ((i + 1) // 2 * 2 - (1 if i % 2 == 0 else 0)) if 0 < i < gx - 1 else i
            far.append((i * gy + j, other * gy + (j if other != i else j ^ 1)))
    outer = [(0, 1), (1, 0), (2, 3), (3, 2)]
    middle = []
    for g in range(gx):
        middle += [(gx + g, 2 * gx + g), (2 * gx + g, gx + g), (g, g ^ 1), (3 * gx + g, 3 * gx + (g ^ 1))]

    term, ku, sent, crossed, held, got = [None] * n, [None] * n, [None] * n, [None] * n, [None] * n, [None] * (n + LAG)
    raws, quots, mass = [None] * n, [None] * n, [None]

    def outward(k, value):
        if maps == 4 and k < n + LAG:
            got[k] = lax.ppermute(value, "map", outer)

    def receive(k):
        if maps == 4:
            (sent[k],) = done(add(term[k], got[k], chain[0]))
            crossed[k] = lax.ppermute(sent[k], ("map", "gx"), middle)

    def total(k):
        if maps == 4:
            later = term[min(k + LAG, n - 1)]
            held[k], passed, mass[0] = done(*add_and_pass(sent[k], crossed[k], later, mass[0], chain[0]))
            outward(k + LAG, passed)
        else:
            held[k] = lax.psum(term[k], "map")
            (mass[0],) = done(*weigh(held[k], mass[0], chain[0]))

    def close(k, name="finish"):
        raws[k], quots[k] = done(*finish(held[k], got[k + LAG], ku[k], chain[0], name))

    def take(first, values):
        for k in range(len(values) // 2):
            term[first + k], ku[first + k] = values[2 * k : 2 * k + 2]
        done(values[0])

    *values, tall, wide, scaling, densities, one = first_chunk(weights, scaling, densities)
    take(0, values)
    outward(0, term[0])
    one = lax.ppermute(one, "gx", near)
    *values, two = inner_chunks(weights, scaling, densities, tall, wide, (one,))
    take(1, values)
    for k in range(1, LAG):
        outward(k, term[k])
    two = lax.ppermute(two, ("gx", "gy"), far)
    receive(0)
    inner_count = rows // WIDE - 2
    receive(1)
    packs = done(*side_pack(scaling, densities, one, two, chain[0]))
    if gy == 2:
        from_left = from_right = lax.ppermute(packs[0], "gy", [(0, 1), (1, 0)])
    else:
        from_left = lax.ppermute(packs[0], "gy", [(i, i + 1) for i in range(gy - 1)])
        from_right = lax.ppermute(packs[1], "gy", [(i + 1, i) for i in range(gy - 1)])
    take(inner_count, edge_chunks(weights, scaling, densities, tall, wide, one, two, chain[0]))
    total(0)
    receive(2)
    total(1)
    receive(3)
    sides = side_chunks(weights, scaling, densities, tall, one, two, from_left, from_right, chain[0])
    take(inner_count + 2, sides)
    total(2)
    for k in range(4, n):
        receive(k)
        total(k - 1)
        close(k - LAG)
    close(n - LAG)
    total(n - 1)
    if maps == 4 and gx == 4 and gy == 2:
        own = mass[0] + lax.ppermute(mass[0], "gy", [(0, 1), (1, 0)])
        own = own + lax.ppermute(own, "gx", near)
        swap = [(i * gx + j, (i ^ 1) * gx + (j ^ 2)) for i in range(4) for j in range(gx)]
        masses = [
            own,
            lax.ppermute(own, ("map", "gx"), swap),
            lax.ppermute(own, "map", outer),
            lax.ppermute(own, "gx", [(i, i ^ 2) for i in range(gx)]),
        ]
        for k in range(n - 3, n):
            close(k, "finish_last")
    else:
        masses = [sum_grid(mass[0], ("gx", "gy"))]
        if maps == 4:
            masses = [jnp.where(in_middle(), masses[0], lax.ppermute(masses[0], "map", outer))]
        for k in range(n - 3, n):
            close(k)
    bary, new = assemble(masses, places, raws, quots, rows, cols, cells)
    return bary, new


def solution(mesh):
    placed = (P("map", "gx", "gy"), P("map", "gx", "gy"), P("map"))
    return jax.shard_map(
        local,
        mesh=mesh,
        in_specs=placed,
        out_specs=(P("gx", "gy"), P("map", "gx", "gy")),
        check_vma=False,
    )
```
